512 devices in a mesh: wide: 64 (over z, y_lo, core), narrow: 8 (over x, y_hi).
Axes of the slice: x: 4, y: 4 (y_hi: 2, y_lo: 2; y = y_hi * 2 + y_lo), z: 16, core: 2. Of those that a mesh axis runs over, the one named last changes fastest.
Arguments:
- queries: bfloat16 [65536, 256], P(('wide', 'narrow')), may hold values from -16 to 16
- hot_table: bfloat16 [2048, 256], replicated, may hold values from -1.5 to 1.5
- cold_table: bfloat16 [16384, 256], P(('wide', 'narrow')), may hold values from -1.25 to 1.25
- hot_ids: int32 [2048], replicated, may hold values from 0 to 18431, as said below
- targets: int32 [65536], replicated, may hold values from 0 to 18431
Outputs:
- grad_queries: bfloat16 [65536, 256], P(('wide', 'narrow'))
- grad_hot: bfloat16 [2048, 256], replicated
- grad_cold: bfloat16 [16384, 256], P(('wide', 'narrow'))
- row_loss: float32 [65536], P(('wide', 'narrow'))
The draws below stay inside these ranges and needn't reach their ends.
Inputs may be any that keep to these rules, and one draw needn't show every extreme that they name: `hot_ids`: 2048 distinct catalogue ids in no particular order.
All inputs are finite; a program needn't handle non-finite values.
Results may differ from the reference program's by a relative error of at most 0.006.
Values may be sent and summed in bfloat16 or wider, within the bound.
No kernel may reach another device: no remote copies, remote signals or barrier semaphores. Data moves between devices by JAX's collectives and lax.ppermute only.
A program may use at most 64 MiB of HBM per device.

```python
import jax
import jax.numpy as jnp
from jax import lax

H = 256
HOT = 2048
QUERIES = 65536
COLD = 16384


def shared_ids(key):
    inner = jax.random.permutation(jax.random.fold_in(key, 72), HOT + COLD - 2)[:HOT - 2] + 1
    listed = jnp.concatenate([jnp.zeros((1,), jnp.int32), jnp.full((1,), HOT + COLD - 1, jnp.int32), inner.astype(jnp.int32)])
    return jax.random.permutation(jax.random.fold_in(key, 73), listed)


def shared_table_common(key):
    return jax.random.normal(jax.random.fold_in(key, 74), (1, H), jnp.float32)


def draw_hot_ids(key, part):
    return shared_ids(key).astype(jnp.int32)


def draw_targets(key, part):
    listed = shared_ids(key)
    key = jax.random.fold_in(key, 3)
    slot_key, any_key, pick_key, end_key = jax.random.split(key, 4)
    slots = jax.random.randint(slot_key, (QUERIES,), 0, HOT)
    anywhere = jax.random.randint(any_key, (QUERIES,), 0, HOT + COLD)
    picks = jax.random.randint(pick_key, (QUERIES,), 0, 2)
    chosen = jnp.where(picks == 1, jnp.take(listed, slots), anywhere)
    ends = jax.random.randint(end_key, (2,), 0, QUERIES // 2)
    positions = jnp.arange(QUERIES)
    chosen = jnp.where(positions == ends[0], 0, chosen)
    chosen = jnp.where(positions == QUERIES // 2 + ends[1], HOT + COLD - 1, chosen)
    return chosen.astype(jnp.int32)


def draw_queries(key, part):
    key = jax.random.fold_in(key, 5)
    noise_key, scale_key, common_key = jax.random.split(key, 3)
    common = jax.random.normal(common_key, (1, H), jnp.float32)
    row_scale = jnp.exp(jax.random.uniform(scale_key, (QUERIES, 1), jnp.float32, jnp.log(0.04), jnp.log(6.0)))
    values = jax.random.normal(noise_key, (QUERIES, H), jnp.float32) * row_scale + 0.3 * common
    return jnp.clip(values, -16.0, 16.0).astype(jnp.bfloat16)


def draw_hot_table(key, part):
    common = shared_table_common(key)
    key = jax.random.fold_in(key, 9)
    noise_key, scale_key = jax.random.split(key, 2)
    row_scale = jnp.exp(jax.random.uniform(scale_key, (HOT, 1), jnp.float32, jnp.log(0.02), jnp.log(0.2)))
    values = jax.random.normal(noise_key, (HOT, H), jnp.float32) * row_scale + 0.1 * common
    return jnp.clip(values, -1.5, 1.5).astype(jnp.bfloat16)


def draw_cold_table(key, part):
    common = shared_table_common(key)
    key = jax.random.fold_in(key, 13)
    noise_key, scale_key = jax.random.split(key, 2)
    row_scale = jnp.exp(jax.random.uniform(scale_key, (COLD, 1), jnp.float32, jnp.log(0.02), jnp.log(0.2)))
    values = jax.random.normal(noise_key, (COLD, H), jnp.float32) * row_scale + 0.1 * common
    return jnp.clip(values, -1.25, 1.25).astype(jnp.bfloat16)


def setup_inputs(seed: int = 0) -> dict:
    key_list = jax.random.split(jax.random.key(seed), 6)
    queries = draw_queries(jax.random.fold_in(key_list[5], 71), 0)
    hot_table = draw_hot_table(jax.random.fold_in(key_list[5], 71), 0)
    cold_table = draw_cold_table(jax.random.fold_in(key_list[5], 71), 0)
    hot_ids = draw_hot_ids(jax.random.fold_in(key_list[5], 71), 0)
    targets = draw_targets(jax.random.fold_in(key_list[5], 71), 0)
    return dict(queries=queries, hot_table=hot_table, cold_table=cold_table, hot_ids=hot_ids, targets=targets)


def decode_targets(hot_ids, targets):
    sorter = jnp.argsort(hot_ids).astype(jnp.int32)
    ordered = jnp.take(hot_ids, sorter)
    below = jnp.searchsorted(ordered, targets).astype(jnp.int32)
    clipped = jnp.minimum(below, hot_ids.shape[0] - 1)
    is_hot = jnp.take(ordered, clipped) == targets
    hot_slot = jnp.take(sorter, clipped)
    return is_hot, hot_slot, targets - below


def reference(queries, hot_table, cold_table, hot_ids, targets):
    is_hot, hot_slot, cold_row = decode_targets(hot_ids, targets)
    hot_column = jnp.where(is_hot, hot_slot, -1).astype(jnp.int32)
    cold_column = jnp.where(is_hot, -1, cold_row).astype(jnp.int32)
    hot_wide = hot_table.astype(jnp.float32)
    cold_wide = cold_table.astype(jnp.float32)
    row_span = min(QUERIES, 2048)
    block_total = QUERIES // row_span

    def row_block(running, pieces):
        grad_hot, grad_cold = running
        query_rows, hot_cols, cold_cols = pieces
        rows_wide = query_rows.astype(jnp.float32)
        hot_scores = jnp.dot(rows_wide, hot_wide.T, preferred_element_type=jnp.float32)
        cold_scores = jnp.dot(rows_wide, cold_wide.T, preferred_element_type=jnp.float32)
        row_top = jnp.maximum(jnp.max(hot_scores, axis=1), jnp.max(cold_scores, axis=1))
        row_sum = jnp.sum(jnp.exp(hot_scores - row_top[:, None]), axis=1) + jnp.sum(jnp.exp(cold_scores - row_top[:, None]), axis=1)
        log_total = row_top + jnp.log(row_sum)
        hot_hit = lax.broadcasted_iota(jnp.int32, hot_scores.shape, 1) == hot_cols[:, None]
        cold_hit = lax.broadcasted_iota(jnp.int32, cold_scores.shape, 1) == cold_cols[:, None]
        hot_weights = lax.optimization_barrier((jnp.exp(hot_scores - log_total[:, None]) - hot_hit.astype(jnp.float32)).astype(jnp.bfloat16)).astype(jnp.float32)
        cold_weights = lax.optimization_barrier((jnp.exp(cold_scores - log_total[:, None]) - cold_hit.astype(jnp.float32)).astype(jnp.bfloat16)).astype(jnp.float32)
        query_grad = jnp.dot(hot_weights, hot_wide, preferred_element_type=jnp.float32) + jnp.dot(cold_weights, cold_wide, preferred_element_type=jnp.float32)
        target_score = jnp.sum(jnp.where(hot_hit, hot_scores, jnp.float32(0.0)), axis=1) + jnp.sum(jnp.where(cold_hit, cold_scores, jnp.float32(0.0)), axis=1)
        grad_hot = grad_hot + jnp.dot(hot_weights.T, rows_wide, preferred_element_type=jnp.float32)
        grad_cold = grad_cold + jnp.dot(cold_weights.T, rows_wide, preferred_element_type=jnp.float32)
        return (grad_hot, grad_cold), (query_grad.astype(jnp.bfloat16), log_total - target_score)

    initial = (jnp.zeros((HOT, H), jnp.float32), jnp.zeros((COLD, H), jnp.float32))
    inputs = (queries.reshape(block_total, row_span, H), hot_column.reshape(block_total, row_span), cold_column.reshape(block_total, row_span))
    (grad_hot, grad_cold), (query_parts, loss_parts) = lax.scan(row_block, initial, inputs)
    return query_parts.reshape(QUERIES, H), grad_hot.astype(jnp.bfloat16), grad_cold.astype(jnp.bfloat16), loss_parts.reshape(QUERIES)
```

```python
import functools

import jax
import jax.numpy as jnp
from jax import lax
from jax.experimental import pallas as pl
from jax.experimental.pallas import tpu as pltpu
from jax.sharding import Mesh
from jax.sharding import PartitionSpec as P

AXES = ("z", "yl", "c", "x2", "x1", "yh")
COLS = ("c", "x2", "yh")
NEAR = ("yl", "x1")
PLANE = COLS + NEAR
BF = jnp.bfloat16
F32 = jnp.float32
NT = (((1,), (1,)), ((), ()))
TN = (((0,), (0,)), ((), ()))


def spread(x, axes):
    n = lax.axis_size(axes)
    return lax.all_to_all(jnp.broadcast_to(x[None], (n, *x.shape)), axes, 0, 0)


def stats_kernel(table_ref, rows_ref, col_ref, out_ref):
    chunks, width, _ = table_ref.shape
    rows = rows_ref[...]
    cols = col_ref[...]
    count = rows.shape[0]

    def step(g, carry):
        top, total, hit = carry
        s = lax.dot_general(table_ref[g], rows, NT, preferred_element_type=F32)
        new = jnp.maximum(top, jnp.max(s, axis=0, keepdims=True))
        total = total * jnp.exp(top - new) + jnp.sum(jnp.exp(s - new), axis=0, keepdims=True)
        where = lax.broadcasted_iota(jnp.int32, s.shape, 0) + g * width == cols
        hit = hit + jnp.sum(jnp.where(where, s, 0.0), axis=0, keepdims=True)
        return new, total, hit

    zero = jnp.zeros((1, count), F32)
    top, total, hit = lax.fori_loop(0, chunks, step, (jnp.full((1, count), -1e30, F32), zero, zero))
    out_ref[0:1] = top
    out_ref[1:2] = total
    out_ref[2:3] = hit
    out_ref[3:8] = jnp.zeros((5, count), F32)


def grads_kernel(table_ref, rows_ref, col_ref, stats_ref, query_ref, item_ref, loss_ref, acc_ref):
    chunks, width, _ = table_ref.shape
    rows = rows_ref[...]
    cols = col_ref[...]
    parts = stats_ref.shape[0]
    tops = [stats_ref[k, 0:1] for k in range(parts)]
    top = functools.reduce(jnp.maximum, tops)
    total = sum(stats_ref[k, 1:2] * jnp.exp(tops[k] - top) for k in range(parts))
    logs = top + jnp.log(total)
    loss_ref[...] = logs - sum(stats_ref[k, 2:3] for k in range(parts))
    acc_ref[...] = jnp.zeros_like(acc_ref)

    def step(g, carry):
        table = table_ref[g]
        s = lax.dot_general(table, rows, NT, preferred_element_type=F32)
        where = lax.broadcasted_iota(jnp.int32, s.shape, 0) + g * width == cols
        w = (jnp.exp(s - logs) - jnp.where(where, 1.0, 0.0)).astype(BF)
        item_ref[g] = jnp.dot(w, rows, preferred_element_type=F32).astype(BF)
        acc_ref[...] += lax.dot_general(table, w, TN, preferred_element_type=F32)
        return carry

    lax.fori_loop(0, chunks, step, 0)
    query_ref[...] = acc_ref[...].T.astype(BF)


def body(queries, hot_table, cold_table, hot_ids, targets):
    own, width = queries.shape
    shard = cold_table.shape[0]
    hot = hot_table.shape[0]
    nz, nc, ng = lax.axis_size("z"), lax.axis_size(COLS), lax.axis_size(NEAR)
    k = lax.axis_index(COLS)
    hot_part = hot // nc
    hot_near = hot_part // ng
    hot_own = hot_near // nz
    near_rows = nz * shard + hot_near

    grouped = spread(queries, COLS).reshape(nc * own, width)
    cold = spread(spread(cold_table, ("z",)).reshape(nz * shard, width), NEAR)
    hot_mine = lax.dynamic_slice_in_dim(hot_table, k * hot_part, hot_part, 0)
    table = jnp.concatenate([cold, hot_mine.reshape(ng, hot_near, width)], axis=1)

    sizes = tuple(lax.axis_size(a) for a in AXES)
    aim = targets.reshape(*sizes, own)
    z, yl, x1 = lax.axis_index("z"), lax.axis_index("yl"), lax.axis_index("x1")
    aim = lax.dynamic_slice(aim, (z, yl, 0, 0, x1, 0, 0), (1, 1, *sizes[2:4], 1, sizes[5], own))
    aim = aim.reshape(1, nc * own)
    ids = hot_ids[:, None]
    below = jnp.sum((ids < aim).astype(jnp.int32), axis=0)
    slot = jnp.sum(
        jnp.where(ids == aim, lax.broadcasted_iota(jnp.int32, (hot, 1), 0) + 1, 0), axis=0
    ) - 1
    hot_k, hot_r = slot // hot_part, slot % hot_part
    hot_col = hot_r // hot_near * near_rows + nz * shard + hot_r % hot_near
    cold_row = aim[0] - below
    block = cold_row // shard
    coord = {}
    for a in reversed(AXES):
        n = lax.axis_size(a)
        coord[a] = block % n
        block = block // n
    cold_k = (coord["c"] * lax.axis_size("x2") + coord["x2"]) * lax.axis_size("yh") + coord["yh"]
    cold_g = coord["yl"] * lax.axis_size("x1") + coord["x1"]
    cold_col = cold_g * near_rows + coord["z"] * shard + cold_row % shard
    is_hot = slot >= 0
    column = jnp.where(is_hot, hot_col, cold_col)
    column = jnp.where(jnp.where(is_hot, hot_k, cold_k) == k, column, -1)[None]

    count = nc * own
    params = pltpu.CompilerParams(vmem_limit_bytes=48 << 20)
    stats = pl.pallas_call(
        stats_kernel,
        out_shape=jax.ShapeDtypeStruct((8, count), F32),
        compiler_params=params,
    )(table, grouped, column)
    stats = spread(stats, COLS)
    query_part, item_part, loss = pl.pallas_call(
        grads_kernel,
        out_shape=(
            jax.ShapeDtypeStruct((count, width), BF),
            jax.ShapeDtypeStruct((ng, near_rows, width), BF),
            jax.ShapeDtypeStruct((1, count), F32),
        ),
        scratch_shapes=[pltpu.VMEM((width, count), F32)],
        compiler_params=params,
    )(table, grouped, column, stats)
    row_loss = lax.dynamic_slice_in_dim(loss[0], k * own, own, 0)

    near = lax.all_to_all(item_part, NEAR, 0, 0)
    near = jnp.sum(near.astype(F32), axis=0).astype(BF)
    cold_near = near[: nz * shard].reshape(nz, shard, width)
    hot_z = near[nz * shard :].reshape(nz, hot_own, width)
    far = lax.all_to_all(jnp.concatenate([cold_near, hot_z], axis=1), ("z",), 0, 0)
    far = jnp.sum(far.astype(F32), axis=0).astype(BF)
    grad_cold = far[:shard]
    grad_hot = spread(far[shard:], ("z",)).reshape(hot_near, width)
    grad_hot = spread(grad_hot, PLANE).reshape(hot, width)

    own_query = lax.all_to_all(query_part.reshape(nc, own, width), COLS, 0, 0)
    grad_queries = jnp.sum(own_query.astype(F32), axis=0).astype(BF)
    return grad_queries, grad_hot, grad_cold, row_loss


def solution(mesh):
    fine = Mesh(mesh.devices.reshape(16, 2, 2, 2, 2, 2), AXES)
    rows = P(AXES, None)
    return jax.shard_map(
        body,
        mesh=fine,
        in_specs=(rows, P(), rows, P(), P()),
        out_specs=(rows, P(), rows, P(AXES)),
        check_vma=False,
    )
```

```python
import functools

import jax
import jax.numpy as jnp
from jax import lax
from jax.experimental import pallas as pl
from jax.experimental.pallas import tpu as pltpu
from jax.sharding import Mesh
from jax.sharding import PartitionSpec as P

AXES = ("z8", "z4", "z2", "z1", "yl", "c", "x2", "x1", "yh")
COLS = ("c", "z1", "z2")
NEAR = ("yl", "x2", "x1", "yh")
FAR = ("z8", "z4")
BF = jnp.bfloat16
F32 = jnp.float32
NT = (((1,), (1,)), ((), ()))
TN = (((0,), (0,)), ((), ()))


def spread(x, axes):
    n = lax.axis_size(axes)
    return lax.all_to_all(jnp.broadcast_to(x[None], (n, *x.shape)), axes, 0, 0)


def swap(x, axis):
    return lax.ppermute(x, axis, [(0, 1), (1, 0)])


def coords(index, order):
    found = {}
    for a in reversed(order):
        found[a] = index % 2
        index = index // 2
    return found


def join(found, order):
    index = 0
    for a in order:
        index = index * 2 + found[a]
    return index


def stats_kernel(k_ref, table_ref, rows_ref, col_ref, out_ref):
    chunks, width, _ = table_ref.shape
    parts = out_ref.shape[1] // 128
    rows = rows_ref[...]
    cols = col_ref[...]
    count = rows.shape[0]
    k = k_ref[0]

    def step(g, carry):
        top, total, hit = carry
        s = lax.dot_general(table_ref[g], rows, NT, preferred_element_type=F32)
        new = jnp.maximum(top, jnp.max(s, axis=0, keepdims=True))
        total = total * jnp.exp(top - new) + jnp.sum(jnp.exp(s - new), axis=0, keepdims=True)
        where = lax.broadcasted_iota(jnp.int32, s.shape, 0) + g * width == cols
        hit = hit + jnp.sum(jnp.where(where, s, 0.0), axis=0, keepdims=True)
        return new, total, hit

    zero = jnp.zeros((1, count), F32)
    top, total, hit = lax.fori_loop(0, chunks, step, (jnp.full((1, count), -1e30, F32), zero, zero))
    for p in range(parts):
        here = slice(p * 128, (p + 1) * 128)
        there = pl.ds(pl.multiple_of((k ^ p) * 128, 128), 128)
        out_ref[0:1, there] = top[:, here]
        out_ref[1:2, there] = total[:, here]
        out_ref[2:3, there] = hit[:, here]
        out_ref[3:8, there] = jnp.zeros((5, 128), F32)


def grads_kernel(
    k_ref, table_ref, rows_ref, col_ref, stats_ref, query_ref, item_ref, loss_ref, acc_ref
):
    chunks, width, _ = table_ref.shape
    rows = rows_ref[...]
    cols = col_ref[...]
    parts = stats_ref.shape[0]
    k = k_ref[0]
    pieces = []
    for p in range(parts):
        there = pl.ds(pl.multiple_of((k ^ p) * 128, 128), 128)
        tops = [stats_ref[d, 0:1, there] for d in range(parts)]
        top = functools.reduce(jnp.maximum, tops)
        total = sum(stats_ref[d, 1:2, there] * jnp.exp(tops[d] - top) for d in range(parts))
        pieces.append(top + jnp.log(total))
        if p == 0:
            loss_ref[...] = pieces[0] - sum(stats_ref[d, 2:3, there] for d in range(parts))
    logs = jnp.concatenate(pieces, axis=1)
    acc_ref[...] = jnp.zeros_like(acc_ref)

    def step(g, carry):
        table = table_ref[g]
        s = lax.dot_general(table, rows, NT, preferred_element_type=F32)
        where = lax.broadcasted_iota(jnp.int32, s.shape, 0) + g * width == cols
        w = (jnp.exp(s - logs) - jnp.where(where, 1.0, 0.0)).astype(BF)
        item_ref[g] = jnp.dot(w, rows, preferred_element_type=F32).astype(BF)
        acc_ref[...] += lax.dot_general(table, w, TN, preferred_element_type=F32)
        return carry

    lax.fori_loop(0, chunks, step, 0)
    query_ref[...] = acc_ref[...].T.astype(BF)


def body(queries, hot_table, cold_table, hot_ids, targets):
    own, width = queries.shape
    shard = cold_table.shape[0]
    hot = hot_table.shape[0]
    nc, ng, nf = 2 ** len(COLS), 2 ** len(NEAR), 2 ** len(FAR)
    hot_own = hot // (nc * ng)
    me = {a: lax.axis_index(a) for a in AXES}
    k = join(me, COLS)

    grouped = queries
    for a in reversed(COLS):
        grouped = jnp.concatenate([grouped, swap(grouped, a)], axis=0)

    far = spread(cold_table, FAR).reshape(nf * shard, width)
    cold = spread(far, NEAR)
    mine = lax.dynamic_index_in_dim(hot_table.reshape(ng, nc, hot_own, width), k, 1, False)
    near_rows = nf * shard + hot_own
    table = jnp.concatenate([cold, mine], axis=1)

    base = join(me, AXES)
    blocks = targets.reshape(-1, own)
    picks = []
    for p in range(nc):
        flip = {a: 0 for a in AXES}
        flip.update(coords(p, COLS))
        picks.append(lax.dynamic_slice_in_dim(blocks, base ^ join(flip, AXES), 1, 0))
    aim = jnp.concatenate(picks, axis=1)
    ids = hot_ids[:, None]
    below = jnp.sum((ids < aim).astype(jnp.int32), axis=0)
    slot = jnp.sum(
        jnp.where(ids == aim, lax.broadcasted_iota(jnp.int32, (hot, 1), 0) + 1, 0), axis=0
    ) - 1
    is_hot = slot >= 0
    cold_row = aim[0] - below
    at = coords(cold_row // shard, AXES)
    hot_block = slot // hot_own
    column = jnp.where(
        is_hot,
        hot_block // nc * near_rows + nf * shard + slot % hot_own,
        join(at, NEAR) * near_rows + join(at, FAR) * shard + cold_row % shard,
    )
    column = jnp.where(jnp.where(is_hot, hot_block % nc, join(at, COLS)) == k, column, -1)[None]

    count = nc * own
    params = pltpu.CompilerParams(vmem_limit_bytes=48 << 20)
    chunks = 4
    table = table.reshape(chunks, ng * near_rows // chunks, width)
    vmem = pl.BlockSpec(memory_space=pltpu.VMEM)
    smem = pl.BlockSpec(memory_space=pltpu.SMEM)
    at_k = jnp.reshape(k, (1,)).astype(jnp.int32)
    stats = pl.pallas_call(
        stats_kernel,
        out_shape=jax.ShapeDtypeStruct((8, count), F32),
        in_specs=[smem, vmem, vmem, vmem],
        compiler_params=params,
    )(at_k, table, grouped, column)
    stats = spread(stats, COLS)
    query_part, item_part, loss = pl.pallas_call(
        grads_kernel,
        out_shape=(
            jax.ShapeDtypeStruct((count, width), BF),
            jax.ShapeDtypeStruct(table.shape, BF),
            jax.ShapeDtypeStruct((1, own), F32),
        ),
        in_specs=[smem, vmem, vmem, vmem, vmem],
        scratch_shapes=[pltpu.VMEM((width, count), F32)],
        compiler_params=params,
    )(at_k, table, grouped, column, stats)

    near = lax.all_to_all(item_part.reshape(ng, near_rows, width), NEAR, 0, 0)
    near = jnp.sum(near.astype(F32), axis=0).astype(BF)
    cold_part = near[: nf * shard].reshape(nf, shard, width)
    hot_part = jnp.broadcast_to(near[None, nf * shard :], (nf, hot_own, width))
    far = lax.all_to_all(jnp.concatenate([cold_part, hot_part], axis=1), FAR, 0, 0)
    far = jnp.sum(far.astype(F32), axis=0).astype(BF)
    grad_cold = far[:shard]
    grad_hot = spread(far[shard:], COLS).reshape(nc * hot_own, width)
    grad_hot = spread(grad_hot, NEAR).reshape(hot, width)

    for a in COLS:
        half = query_part.shape[0] // 2
        other = swap(query_part[half:], a)
        query_part = (query_part[:half].astype(F32) + other.astype(F32)).astype(BF)
    return query_part, grad_hot, grad_cold, loss[0]


def solution(mesh):
    fine = Mesh(mesh.devices.reshape((2,) * len(AXES)), AXES)
    rows = P(AXES, None)
    return jax.shard_map(
        body,
        mesh=fine,
        in_specs=(rows, P(), rows, P(), P()),
        out_specs=(rows, P(), rows, P(AXES)),
        check_vma=False,
    )
```

```python
import functools

import jax
import jax.numpy as jnp
from jax import lax
from jax.experimental import pallas as pl
from jax.experimental.pallas import tpu as pltpu
from jax.sharding import Mesh
from jax.sharding import PartitionSpec as P

AXES = ("z8", "z4", "z2", "z1", "yl", "c", "x2", "x1", "yh")
COLS = ("c", "z1", "z2")
NEAR = ("yl", "x2", "x1", "yh")
FAR = ("z8", "z4")
NC, NG, NF = 2 ** len(COLS), 2 ** len(NEAR), 2 ** len(FAR)
BF = jnp.bfloat16
F32 = jnp.float32
NT = (((1,), (1,)), ((), ()))
TN = (((0,), (0,)), ((), ()))
CHUNKS = 4


def spread(x, axes):
    n = lax.axis_size(axes)
    return lax.all_to_all(jnp.broadcast_to(x[None], (n, *x.shape)), axes, 0, 0)


def swap(x, axis):
    return lax.ppermute(x, axis, [(0, 1), (1, 0)])


def bit(index, axis):
    return (index >> (len(AXES) - 1 - AXES.index(axis))) & 1


def pick(index, axes):
    out = 0
    for a in axes:
        out = out * 2 + bit(index, a)
    return out


def flip(p):
    mask = 0
    for a in reversed(COLS):
        mask |= (p & 1) << (len(AXES) - 1 - AXES.index(a))
        p >>= 1
    return mask


def decode_kernel(me_ref, ids_ref, targets_ref, out_ref):
    me = me_ref[0]
    k = pick(me, COLS)
    groups, lanes = ids_ref.shape
    own = targets_ref.shape[1]
    hot_own = groups * lanes // (NC * NG)
    shard = 32
    near_chunk = NG // CHUNKS
    width = near_chunk * (NF * shard + hot_own)
    aim = jnp.concatenate([targets_ref[pl.ds(me ^ flip(p), 1)] for p in range(NC)], axis=1)
    below = jnp.zeros(aim.shape, jnp.int32)
    slot = jnp.zeros(aim.shape, jnp.int32)
    for i in range(groups):
        ids = jnp.broadcast_to(ids_ref[i : i + 1], (lanes, lanes)).T
        ids = jnp.concatenate([ids] * NC, axis=1)
        place = lax.broadcasted_iota(jnp.int32, ids.shape, 0) + (i * lanes + 1)
        below += jnp.sum((ids < aim).astype(jnp.int32), axis=0, keepdims=True)
        slot += jnp.sum(jnp.where(ids == aim, place, 0), axis=0, keepdims=True)
    slot -= 1
    is_hot = slot >= 0
    row = aim - below
    block = row >> 5
    near = pick(block, NEAR)
    cold_col = near // near_chunk * width + (near % near_chunk) * (NF * shard)
    cold_col += pick(block, FAR) * shard + (row & (shard - 1))
    hot_block = slot >> 4
    hot_near = hot_block >> 3
    hot_col = hot_near // near_chunk * width + near_chunk * NF * shard
    hot_col += (hot_near % near_chunk) * hot_own + (slot & (hot_own - 1))
    column = jnp.where(is_hot, hot_col, cold_col)
    there = jnp.where(is_hot, hot_block & (NC - 1), pick(block, COLS))
    out_ref[...] = jnp.where(there == k, column, -1)


def chunk_table(cold_ref, hot_ref, g):
    n = NG // CHUNKS
    cold = cold_ref[pl.ds(g * n, n)]
    hot = hot_ref[pl.ds(g * n, n)]
    wide = cold.shape[-1]
    return jnp.concatenate([cold.reshape(-1, wide), hot.reshape(-1, wide)], axis=0)


def stats_kernel(me_ref, cold_ref, hot_ref, col_ref, *refs):
    *row_refs, out_ref = refs
    rows = jnp.concatenate([r[...] for r in row_refs], axis=0)
    cols = col_ref[...]
    count = rows.shape[0]
    k = pick(me_ref[0], COLS)

    def step(g, carry):
        top, total, hit = carry
        table = chunk_table(cold_ref, hot_ref, g)
        s = lax.dot_general(table, rows, NT, preferred_element_type=F32)
        new = jnp.maximum(top, jnp.max(s, axis=0, keepdims=True))
        total = total * jnp.exp(top - new) + jnp.sum(jnp.exp(s - new), axis=0, keepdims=True)
        where = lax.broadcasted_iota(jnp.int32, s.shape, 0) == cols - g * table.shape[0]
        hit = hit + jnp.sum(jnp.where(where, s, 0.0), axis=0, keepdims=True)
        return new, total, hit

    zero = jnp.zeros((1, count), F32)
    top, total, hit = lax.fori_loop(0, CHUNKS, step, (jnp.full((1, count), -1e30, F32), zero, zero))
    for p in range(NC):
        here = slice(p * 128, (p + 1) * 128)
        there = pl.ds(pl.multiple_of((k ^ p) * 128, 128), 128)
        out_ref[0:1, there] = top[:, here]
        out_ref[1:2, there] = total[:, here]
        out_ref[2:3, there] = hit[:, here]
        out_ref[3:4, there] = jnp.zeros((1, 128), F32)


def grads_kernel(me_ref, cold_ref, hot_ref, col_ref, stats_ref, *refs):
    *row_refs, keep_ref, send_ref, item_ref, loss_ref, acc_ref = refs
    rows = jnp.concatenate([r[...] for r in row_refs], axis=0)
    cols = col_ref[...]
    k = pick(me_ref[0], COLS)
    pieces = []
    for p in range(NC):
        there = pl.ds(pl.multiple_of((k ^ p) * 128, 128), 128)
        tops = [stats_ref[d, 0:1, there] for d in range(NC)]
        top = functools.reduce(jnp.maximum, tops)
        total = sum(stats_ref[d, 1:2, there] * jnp.exp(tops[d] - top) for d in range(NC))
        pieces.append(top + jnp.log(total))
        if p == 0:
            loss_ref[...] = pieces[0] - sum(stats_ref[d, 2:3, there] for d in range(NC))
    logs = jnp.concatenate(pieces, axis=1)
    acc_ref[...] = jnp.zeros_like(acc_ref)
    n = NG // CHUNKS
    cold_rows = cold_ref.shape[1]

    def step(g, carry):
        table = chunk_table(cold_ref, hot_ref, g)
        s = lax.dot_general(table, rows, NT, preferred_element_type=F32)
        where = lax.broadcasted_iota(jnp.int32, s.shape, 0) == cols - g * table.shape[0]
        w = (jnp.exp(s - logs) - jnp.where(where, 1.0, 0.0)).astype(BF)
        item = jnp.dot(w, rows, preferred_element_type=F32).astype(BF)
        wide = item.shape[-1]
        item_ref[pl.ds(g * n, n), :cold_rows] = item[: n * cold_rows].reshape(n, -1, wide)
        item_ref[pl.ds(g * n, n), cold_rows:] = item[n * cold_rows :].reshape(n, -1, wide)
        acc_ref[...] += lax.dot_general(table, w, TN, preferred_element_type=F32)
        return carry

    lax.fori_loop(0, CHUNKS, step, 0)
    half = acc_ref.shape[1] // 2
    keep_ref[...] = acc_ref[:, :half].T
    send_ref[...] = acc_ref[:, half:].T


def body(queries, hot_table, cold_table, hot_ids, targets):
    own, width = queries.shape
    shard = cold_table.shape[0]
    hot = hot_table.shape[0]
    hot_own = hot // (NC * NG)
    me = lax.axis_index(AXES)
    at_me = jnp.reshape(me, (1,)).astype(jnp.int32)
    k = pick(me, COLS)
    count = NC * own
    params = pltpu.CompilerParams(vmem_limit_bytes=48 << 20)
    vmem = pl.BlockSpec(memory_space=pltpu.VMEM)
    smem = pl.BlockSpec(memory_space=pltpu.SMEM)

    column = pl.pallas_call(
        decode_kernel,
        out_shape=jax.ShapeDtypeStruct((1, count), jnp.int32),
        in_specs=[smem, vmem, vmem],
        cost_estimate=pl.CostEstimate(flops=6 * hot * count, bytes_accessed=1 << 19, transcendentals=0),
        compiler_params=params,
    )(at_me, hot_ids.reshape(-1, 128), targets.reshape(-1, own))

    rows = [queries]
    for a in reversed(COLS):
        rows.append(swap(jnp.concatenate(rows, axis=0), a))

    far = spread(cold_table, FAR).reshape(NF * shard, width)
    far, rows[1], rows[2] = lax.optimization_barrier((far, rows[1], rows[2]))
    cold = spread(far, NEAR)
    mine = lax.dynamic_index_in_dim(hot_table.reshape(NG, NC, hot_own, width), k, 1, False)

    stats = pl.pallas_call(
        stats_kernel,
        out_shape=jax.ShapeDtypeStruct((4, count), F32),
        in_specs=[smem] + [vmem] * (3 + len(rows)),
        compiler_params=params,
    )(at_me, cold, mine, column, *rows)
    stats = spread(stats, COLS)
    keep, send, item_part, loss = pl.pallas_call(
        grads_kernel,
        out_shape=(
            jax.ShapeDtypeStruct((count // 2, width), F32),
            jax.ShapeDtypeStruct((count // 2, width), F32),
            jax.ShapeDtypeStruct((NG, NF * shard + hot_own, width), BF),
            jax.ShapeDtypeStruct((1, own), F32),
        ),
        in_specs=[smem] + [vmem] * (4 + len(rows)),
        scratch_shapes=[pltpu.VMEM((width, count), F32)],
        compiler_params=params,
    )(at_me, cold, mine, column, stats, *rows)

    near = lax.all_to_all(item_part, NEAR, 0, 0)
    other = swap(send, COLS[0])
    near, other = lax.optimization_barrier((near, other))
    keep = keep + other
    near = jnp.sum(near.astype(F32), axis=0).astype(BF)
    cold_part = near[: NF * shard].reshape(NF, shard, width)
    hot_part = jnp.broadcast_to(near[None, NF * shard :], (NF, hot_own, width))
    far = lax.all_to_all(jnp.concatenate([cold_part, hot_part], axis=1), FAR, 0, 0)
    other = swap(keep[count // 4 :], COLS[1])
    far, other = lax.optimization_barrier((far, other))
    keep = keep[: count // 4] + other
    far = jnp.sum(far.astype(F32), axis=0).astype(BF)
    grad_cold = far[:shard]
    grad_hot = spread(far[shard:], COLS)
    other = swap(keep[own:], COLS[2])
    grad_hot, other = lax.optimization_barrier((grad_hot, other))
    grad_queries = (keep[:own] + other).astype(BF)
    grad_hot = spread(grad_hot.reshape(NC * hot_own, width), NEAR).reshape(hot, width)
    return grad_queries, grad_hot, grad_cold, loss[0]


def solution(mesh):
    fine = Mesh(mesh.devices.reshape((2,) * len(AXES)), AXES)
    rows = P(AXES, None)
    return jax.shard_map(
        body,
        mesh=fine,
        in_specs=(rows, P(), rows, P(), P()),
        out_specs=(rows, P(), rows, P(AXES)),
        check_vma=False,
    )
```

```python
import functools

import jax
import jax.numpy as jnp
from jax import lax
from jax.experimental import pallas as pl
from jax.experimental.pallas import tpu as pltpu
from jax.sharding import Mesh
from jax.sharding import PartitionSpec as P

AXES = ("z8", "z4", "z2", "z1", "yl", "c", "x2", "x1", "yh")
COLS = ("z1", "z2", "yl", "c")
HALF = ("z1", "z2", "yl")
NEAR = ("x2", "x1", "yh")
FAR = ("z8", "z4")
NC, NG, NF = 2 ** len(COLS), 2 ** len(NEAR), 2 ** len(FAR)
BF = jnp.bfloat16
F32 = jnp.float32
NT = (((1,), (1,)), ((), ()))
TN = (((0,), (0,)), ((), ()))
CHUNKS = 4


def spread(x, axes):
    n = lax.axis_size(axes)
    return lax.all_to_all(jnp.broadcast_to(x[None], (n, *x.shape)), axes, 0, 0)


def swap(x, axis):
    return lax.ppermute(x, axis, [(0, 1), (1, 0)])


def bit(index, axis):
    return (index >> (len(AXES) - 1 - AXES.index(axis))) & 1


def pick(index, axes):
    out = 0
    for a in axes:
        out = out * 2 + bit(index, a)
    return out


def flip(p):
    mask = 0
    for a in reversed(COLS):
        mask |= (p & 1) << (len(AXES) - 1 - AXES.index(a))
        p >>= 1
    return mask


def decode_kernel(me_ref, ids_ref, targets_ref, out_ref):
    me = me_ref[0]
    k = pick(me, COLS)
    groups, lanes = ids_ref.shape
    own = targets_ref.shape[1]
    hot_own = groups * lanes // (NC * NG)
    shard = 32
    near_chunk = NG // CHUNKS
    width = near_chunk * (NF * shard + hot_own)
    aim = jnp.concatenate([targets_ref[pl.ds(me ^ flip(p), 1)] for p in range(NC)], axis=1)
    below = jnp.zeros(aim.shape, jnp.int32)
    slot = jnp.zeros(aim.shape, jnp.int32)
    for i in range(groups):
        ids = jnp.broadcast_to(ids_ref[i : i + 1], (lanes, lanes)).T
        ids = jnp.concatenate([ids] * NC, axis=1)
        place = lax.broadcasted_iota(jnp.int32, ids.shape, 0) + (i * lanes + 1)
        below += jnp.sum((ids < aim).astype(jnp.int32), axis=0, keepdims=True)
        slot += jnp.sum(jnp.where(ids == aim, place, 0), axis=0, keepdims=True)
    slot -= 1
    is_hot = slot >= 0
    row = aim - below
    block = row >> 5
    near = pick(block, NEAR)
    cold_col = near // near_chunk * width + (near % near_chunk) * (NF * shard)
    cold_col += pick(block, FAR) * shard + (row & (shard - 1))
    hot_near = (slot >> 7) & (NG - 1)
    hot_k = (((slot >> 4) & 7) << 1) | (slot >> 10)
    hot_col = hot_near // near_chunk * width + near_chunk * NF * shard
    hot_col += (hot_near % near_chunk) * hot_own + (slot & (hot_own - 1))
    column = jnp.where(is_hot, hot_col, cold_col)
    there = jnp.where(is_hot, hot_k, pick(block, COLS))
    out_ref[...] = jnp.where(there == k, column, -1)


def chunk_table(cold_ref, hot_ref, g):
    n = NG // CHUNKS
    cold = cold_ref[pl.ds(g * n, n)]
    hot = hot_ref[pl.ds(g * n, n)]
    wide = cold.shape[-1]
    return jnp.concatenate([cold.reshape(-1, wide), hot.reshape(-1, wide)], axis=0)


def stats_kernel(me_ref, cold_ref, hot_ref, col_ref, *refs):
    *row_refs, out_ref = refs
    rows = jnp.concatenate([r[...] for r in row_refs], axis=0)
    cols = col_ref[...]
    count = rows.shape[0]
    k = pick(me_ref[0], COLS)

    def step(g, carry):
        top, total, hit = carry
        table = chunk_table(cold_ref, hot_ref, g)
        s = lax.dot_general(table, rows, NT, preferred_element_type=F32)
        new = jnp.maximum(top, jnp.max(s, axis=0, keepdims=True))
        total = total * jnp.exp(top - new) + jnp.sum(jnp.exp(s - new), axis=0, keepdims=True)
        where = lax.broadcasted_iota(jnp.int32, s.shape, 0) == cols - g * table.shape[0]
        hit = hit + jnp.sum(jnp.where(where, s, 0.0), axis=0, keepdims=True)
        return new, total, hit

    zero = jnp.zeros((1, count), F32)
    top, total, hit = lax.fori_loop(0, CHUNKS, step, (jnp.full((1, count), -1e30, F32), zero, zero))
    logs = top + jnp.log(total)
    for p in range(NC):
        here = slice(p * 128, (p + 1) * 128)
        there = pl.ds(pl.multiple_of((k ^ p) * 128, 128), 128)
        out_ref[0:1, there] = logs[:, here]
        out_ref[1:2, there] = hit[:, here]


def grads_kernel(me_ref, cold_ref, hot_ref, col_ref, stats_ref, *refs):
    *row_refs, keep_ref, send_ref, item_ref, loss_ref, acc_ref = refs
    rows = jnp.concatenate([r[...] for r in row_refs], axis=0)
    cols = col_ref[...]
    k = pick(me_ref[0], COLS)
    pieces = []
    for p in range(NC):
        there = pl.ds(pl.multiple_of((k ^ p) * 128, 128), 128)
        tops = [stats_ref[d, 0:1, there] for d in range(NC)]
        top = functools.reduce(jnp.maximum, tops)
        total = sum(jnp.exp(t - top) for t in tops)
        pieces.append(top + jnp.log(total))
        if p == 0:
            loss_ref[...] = pieces[0] - sum(stats_ref[d, 1:2, there] for d in range(NC))
    logs = jnp.concatenate(pieces, axis=1)
    acc_ref[...] = jnp.zeros_like(acc_ref)
    n = NG // CHUNKS
    cold_rows = cold_ref.shape[1]

    def step(g, carry):
        table = chunk_table(cold_ref, hot_ref, g)
        s = lax.dot_general(table, rows, NT, preferred_element_type=F32)
        where = lax.broadcasted_iota(jnp.int32, s.shape, 0) == cols - g * table.shape[0]
        w = (jnp.exp(s - logs) - jnp.where(where, 1.0, 0.0)).astype(BF)
        item = jnp.dot(w, rows, preferred_element_type=F32).astype(BF)
        wide = item.shape[-1]
        item_ref[pl.ds(g * n, n), :cold_rows] = item[: n * cold_rows].reshape(n, -1, wide)
        item_ref[pl.ds(g * n, n), cold_rows:] = item[n * cold_rows :].reshape(n, -1, wide)
        acc_ref[...] += lax.dot_general(table, w, TN, preferred_element_type=F32)
        return carry

    lax.fori_loop(0, CHUNKS, step, 0)
    for j in range(NC // 2):
        out = slice(j * 128, (j + 1) * 128)
        keep_ref[out] = acc_ref[:, 2 * j * 128 : (2 * j + 1) * 128].T
        send_ref[out] = acc_ref[:, (2 * j + 1) * 128 : (2 * j + 2) * 128].T.astype(BF)


def place_kernel(me_ref, own_ref, other_ref, out_ref, sems):
    core = bit(me_ref[0], "c")
    half = own_ref.shape[0]
    first = pltpu.make_async_copy(own_ref, out_ref.at[pl.ds(core * half, half)], sems.at[0])
    second = pltpu.make_async_copy(
        other_ref, out_ref.at[pl.ds((1 - core) * half, half)], sems.at[1]
    )
    first.start()
    second.start()
    first.wait()
    second.wait()


def body(queries, hot_table, cold_table, hot_ids, targets):
    own, width = queries.shape
    shard = cold_table.shape[0]
    hot = hot_table.shape[0]
    hot_own = hot // (NC * NG)
    me = lax.axis_index(AXES)
    at_me = jnp.reshape(me, (1,)).astype(jnp.int32)
    k = pick(me, COLS)
    count = NC * own
    params = pltpu.CompilerParams(vmem_limit_bytes=24 << 20)
    vmem = pl.BlockSpec(memory_space=pltpu.VMEM)
    smem = pl.BlockSpec(memory_space=pltpu.SMEM)

    column = pl.pallas_call(
        decode_kernel,
        out_shape=jax.ShapeDtypeStruct((1, count), jnp.int32),
        in_specs=[smem, vmem, vmem],
        cost_estimate=pl.CostEstimate(flops=6 * hot * count, bytes_accessed=1 << 19, transcendentals=0),
        compiler_params=params,
    )(at_me, hot_ids.reshape(-1, 128), targets.reshape(-1, own))

    pair = jnp.concatenate([queries, swap(queries, "c")], axis=0)
    rows = [pair, swap(pair, "yl"), swap(pair, "z2")]
    rows.append(lax.ppermute(pair, ("z2", "yl"), [(i, 3 - i) for i in range(4)]))

    far = spread(cold_table, FAR).reshape(NF * shard, width)
    far, rows = lax.optimization_barrier((far, jnp.concatenate(rows, axis=0)))
    cold = spread(far, NEAR)
    rows = [rows, swap(rows, "z1")]
    mine = hot_table.reshape(2, NG, NC // 2, hot_own, width)
    mine = lax.dynamic_slice(mine, (k & 1, 0, k >> 1, 0, 0), (1, NG, 1, hot_own, width))
    mine = mine.reshape(NG, hot_own, width)

    stats = pl.pallas_call(
        stats_kernel,
        out_shape=jax.ShapeDtypeStruct((2, count), F32),
        in_specs=[smem] + [vmem] * (3 + len(rows)),
        compiler_params=params,
    )(at_me, cold, mine, column, *rows)
    stats = spread(stats, COLS)
    keep, send, item_part, loss = pl.pallas_call(
        grads_kernel,
        out_shape=(
            jax.ShapeDtypeStruct((count // 2, width), F32),
            jax.ShapeDtypeStruct((count // 2, width), BF),
            jax.ShapeDtypeStruct((NG, NF * shard + hot_own, width), BF),
            jax.ShapeDtypeStruct((1, own), F32),
        ),
        in_specs=[smem] + [vmem] * (4 + len(rows)),
        scratch_shapes=[pltpu.VMEM((width, count), F32)],
        compiler_params=params,
    )(at_me, cold, mine, column, stats, *rows)

    near = lax.all_to_all(item_part, NEAR, 0, 0)
    keep = keep + swap(send, "c").astype(F32)
    other = swap(keep[count // 4 :].astype(BF), "z1")
    near, other = lax.optimization_barrier((near, other))
    near = jnp.sum(near.astype(F32), axis=0).astype(BF)
    cold_part = near[: NF * shard].reshape(NF, shard, width)
    hot_part = jnp.broadcast_to(near[None, NF * shard :], (NF, hot_own, width))
    far = lax.all_to_all(jnp.concatenate([cold_part, hot_part], axis=1), FAR, 0, 0)
    far = jnp.sum(far.astype(F32), axis=0).astype(BF)
    grad_cold = far[:shard]
    keep = keep[: count // 4] + other.astype(F32)
    for a in ("z2", "yl"):
        half = keep.shape[0] // 2
        keep = keep[:half] + swap(keep[half:].astype(BF), a).astype(F32)
    grad_hot = spread(far[shard:], HALF).reshape(-1, width)
    grad_hot = spread(grad_hot, NEAR)
    grad_hot, keep = lax.optimization_barrier((grad_hot, keep))
    grad_hot = grad_hot.reshape(hot // 2, width)
    grad_hot = pl.pallas_call(
        place_kernel,
        out_shape=jax.ShapeDtypeStruct((hot, width), BF),
        in_specs=[smem, vmem, vmem],
        out_specs=pl.BlockSpec(memory_space=pl.ANY),
        scratch_shapes=[pltpu.SemaphoreType.DMA((2,))],
        compiler_params=params,
    )(at_me, grad_hot, swap(grad_hot, "c"))
    return keep.astype(BF), grad_hot, grad_cold, loss[0]


def solution(mesh):
    fine = Mesh(mesh.devices.reshape((2,) * len(AXES)), AXES)
    rows = P(AXES, None)
    return jax.shard_map(
        body,
        mesh=fine,
        in_specs=(rows, P(), rows, P(), P()),
        out_specs=(rows, P(), rows, P(AXES)),
        check_vma=False,
    )
```

```python
import functools

import jax
import jax.numpy as jnp
from jax import lax
from jax.experimental import pallas as pl
from jax.experimental.pallas import tpu as pltpu
from jax.sharding import Mesh
from jax.sharding import PartitionSpec as P

AXES = ("z8", "z4", "z2", "z1", "yl", "c", "x2", "x1", "yh")
COLS = ("c", "z1", "z2")
HALF = ("z1", "z2")
NEAR = ("yl", "x2", "x1", "yh")
FAR = ("z8", "z4")
NC, NG, NF = 2 ** len(COLS), 2 ** len(NEAR), 2 ** len(FAR)
BF = jnp.bfloat16
F32 = jnp.float32
NT = (((1,), (1,)), ((), ()))
TN = (((0,), (0,)), ((), ()))
CHUNKS = 4


def spread(x, axes):
    n = lax.axis_size(axes)
    return lax.all_to_all(jnp.broadcast_to(x[None], (n, *x.shape)), axes, 0, 0)


def swap(x, axis):
    return lax.ppermute(x, axis, [(0, 1), (1, 0)])


def bit(index, axis):
    return (index >> (len(AXES) - 1 - AXES.index(axis))) & 1


def pick(index, axes):
    out = 0
    for a in axes:
        out = out * 2 + bit(index, a)
    return out


def flip(p):
    mask = 0
    for a in reversed(COLS):
        mask |= (p & 1) << (len(AXES) - 1 - AXES.index(a))
        p >>= 1
    return mask


def decode_kernel(me_ref, ids_ref, targets_ref, out_ref):
    me = me_ref[0]
    k = pick(me, COLS)
    groups, lanes = ids_ref.shape
    own = targets_ref.shape[1]
    hot_own = groups * lanes // (NC * NG)
    shard = 32
    near_chunk = NG // CHUNKS
    width = near_chunk * (NF * shard + hot_own)
    aim = jnp.concatenate([targets_ref[pl.ds(me ^ flip(p), 1)] for p in range(NC)], axis=1)
    below = jnp.zeros(aim.shape, jnp.int32)
    slot = jnp.zeros(aim.shape, jnp.int32)
    for i in range(groups):
        ids = jnp.broadcast_to(ids_ref[i : i + 1], (lanes, lanes)).T
        ids = jnp.concatenate([ids] * NC, axis=1)
        place = lax.broadcasted_iota(jnp.int32, ids.shape, 0) + (i * lanes + 1)
        below += jnp.sum((ids < aim).astype(jnp.int32), axis=0, keepdims=True)
        slot += jnp.sum(jnp.where(ids == aim, place, 0), axis=0, keepdims=True)
    slot -= 1
    is_hot = slot >= 0
    row = aim - below
    block = row >> 5
    near = pick(block, NEAR)
    cold_col = near // near_chunk * width + (near % near_chunk) * (NF * shard)
    cold_col += pick(block, FAR) * shard + (row & (shard - 1))
    hot_near = (slot >> 6) & (NG - 1)
    hot_k = ((slot >> 10) << 2) | ((slot >> 4) & 3)
    hot_col = hot_near // near_chunk * width + near_chunk * NF * shard
    hot_col += (hot_near % near_chunk) * hot_own + (slot & (hot_own - 1))
    column = jnp.where(is_hot, hot_col, cold_col)
    there = jnp.where(is_hot, hot_k, pick(block, COLS))
    out_ref[...] = jnp.where(there == k, column, -1)


def chunk_table(cold_ref, hot_ref, g):
    n = NG // CHUNKS
    cold = cold_ref[pl.ds(g * n, n)]
    hot = hot_ref[pl.ds(g * n, n)]
    wide = cold.shape[-1]
    return jnp.concatenate([cold.reshape(-1, wide), hot.reshape(-1, wide)], axis=0)


def stats_kernel(me_ref, cold_ref, hot_ref, col_ref, *refs):
    *row_refs, out_ref = refs
    rows = jnp.concatenate([r[...] for r in row_refs], axis=0)
    cols = col_ref[...]
    count = rows.shape[0]
    k = pick(me_ref[0], COLS)

    def step(g, carry):
        top, total, hit = carry
        table = chunk_table(cold_ref, hot_ref, g)
        s = lax.dot_general(table, rows, NT, preferred_element_type=F32)
        new = jnp.maximum(top, jnp.max(s, axis=0, keepdims=True))
        total = total * jnp.exp(top - new) + jnp.sum(jnp.exp(s - new), axis=0, keepdims=True)
        where = lax.broadcasted_iota(jnp.int32, s.shape, 0) == cols - g * table.shape[0]
        hit = hit + jnp.sum(jnp.where(where, s, 0.0), axis=0, keepdims=True)
        return new, total, hit

    zero = jnp.zeros((1, count), F32)
    top, total, hit = lax.fori_loop(0, CHUNKS, step, (jnp.full((1, count), -1e30, F32), zero, zero))
    logs = top + jnp.log(total)
    for p in range(NC):
        here = slice(p * 128, (p + 1) * 128)
        there = pl.ds(pl.multiple_of((k ^ p) * 128, 128), 128)
        out_ref[0:1, there] = logs[:, here]
        out_ref[1:2, there] = hit[:, here]


def grads_kernel(me_ref, cold_ref, hot_ref, col_ref, stats_ref, *refs):
    *row_refs, keep_ref, send_ref, item_ref, loss_ref, acc_ref = refs
    rows = jnp.concatenate([r[...] for r in row_refs], axis=0)
    cols = col_ref[...]
    k = pick(me_ref[0], COLS)
    pieces = []
    for p in range(NC):
        there = pl.ds(pl.multiple_of((k ^ p) * 128, 128), 128)
        tops = [stats_ref[d, 0:1, there] for d in range(NC)]
        top = functools.reduce(jnp.maximum, tops)
        total = sum(jnp.exp(t - top) for t in tops)
        pieces.append(top + jnp.log(total))
        if p == 0:
            loss_ref[...] = pieces[0] - sum(stats_ref[d, 1:2, there] for d in range(NC))
    logs = jnp.concatenate(pieces, axis=1)
    acc_ref[...] = jnp.zeros_like(acc_ref)
    n = NG // CHUNKS
    cold_rows = cold_ref.shape[1]

    def step(g, carry):
        table = chunk_table(cold_ref, hot_ref, g)
        s = lax.dot_general(table, rows, NT, preferred_element_type=F32)
        where = lax.broadcasted_iota(jnp.int32, s.shape, 0) == cols - g * table.shape[0]
        w = (jnp.exp(s - logs) - jnp.where(where, 1.0, 0.0)).astype(BF)
        item = jnp.dot(w, rows, preferred_element_type=F32).astype(BF)
        wide = item.shape[-1]
        item_ref[pl.ds(g * n, n), :cold_rows] = item[: n * cold_rows].reshape(n, -1, wide)
        item_ref[pl.ds(g * n, n), cold_rows:] = item[n * cold_rows :].reshape(n, -1, wide)
        acc_ref[...] += lax.dot_general(table, w, TN, preferred_element_type=F32)
        return carry

    lax.fori_loop(0, CHUNKS, step, 0)
    half = acc_ref.shape[1] // 2
    keep_ref[...] = acc_ref[:, :half].T
    send_ref[...] = acc_ref[:, half:].T.astype(BF)


def place_kernel(me_ref, own_ref, other_ref, out_ref, sems):
    core = bit(me_ref[0], "c")
    half = own_ref.shape[0]
    first = pltpu.make_async_copy(own_ref, out_ref.at[pl.ds(core * half, half)], sems.at[0])
    second = pltpu.make_async_copy(
        other_ref, out_ref.at[pl.ds((1 - core) * half, half)], sems.at[1]
    )
    first.start()
    second.start()
    first.wait()
    second.wait()


def body(queries, hot_table, cold_table, hot_ids, targets):
    own, width = queries.shape
    shard = cold_table.shape[0]
    hot = hot_table.shape[0]
    hot_own = hot // (NC * NG)
    me = lax.axis_index(AXES)
    at_me = jnp.reshape(me, (1,)).astype(jnp.int32)
    k = pick(me, COLS)
    count = NC * own
    params = pltpu.CompilerParams(vmem_limit_bytes=24 << 20)
    vmem = pl.BlockSpec(memory_space=pltpu.VMEM)
    smem = pl.BlockSpec(memory_space=pltpu.SMEM)

    column = pl.pallas_call(
        decode_kernel,
        out_shape=jax.ShapeDtypeStruct((1, count), jnp.int32),
        in_specs=[smem, vmem, vmem],
        cost_estimate=pl.CostEstimate(flops=6 * hot * count, bytes_accessed=1 << 19, transcendentals=0),
        compiler_params=params,
    )(at_me, hot_ids.reshape(-1, 128), targets.reshape(-1, own))

    rows = [queries, swap(queries, "z2")]

    far = spread(cold_table, FAR).reshape(NF * shard, width)
    far, rows[1], column = lax.optimization_barrier((far, rows[1], column))
    cold = spread(far, NEAR)
    for a in ("z1", "c"):
        rows.append(swap(jnp.concatenate(rows, axis=0), a))
    mine = hot_table.reshape(2, NG, NC // 2, hot_own, width)
    mine = lax.dynamic_slice(mine, (k >> 2, 0, k & 3, 0, 0), (1, NG, 1, hot_own, width))
    mine = mine.reshape(NG, hot_own, width)

    stats = pl.pallas_call(
        stats_kernel,
        out_shape=jax.ShapeDtypeStruct((2, count), F32),
        in_specs=[smem] + [vmem] * (3 + len(rows)),
        compiler_params=params,
    )(at_me, cold, mine, column, *rows)
    stats = spread(stats, COLS)
    keep, send, item_part, loss = pl.pallas_call(
        grads_kernel,
        out_shape=(
            jax.ShapeDtypeStruct((count // 2, width), F32),
            jax.ShapeDtypeStruct((count // 2, width), BF),
            jax.ShapeDtypeStruct((NG, NF * shard + hot_own, width), BF),
            jax.ShapeDtypeStruct((1, own), F32),
        ),
        in_specs=[smem] + [vmem] * (4 + len(rows)),
        scratch_shapes=[pltpu.VMEM((width, count), F32)],
        compiler_params=params,
    )(at_me, cold, mine, column, stats, *rows)

    near = lax.all_to_all(item_part, NEAR, 0, 0)
    keep = keep + swap(send, "c").astype(F32)
    other = swap(keep[count // 4 :].astype(BF), "z1")
    near, other = lax.optimization_barrier((near, other))
    near = jnp.sum(near.astype(F32), axis=0).astype(BF)
    cold_part = near[: NF * shard].reshape(NF, shard, width)
    hot_part = jnp.broadcast_to(near[None, NF * shard :], (NF, hot_own, width))
    far = lax.all_to_all(jnp.concatenate([cold_part, hot_part], axis=1), FAR, 0, 0)
    far = jnp.sum(far.astype(F32), axis=0).astype(BF)
    grad_cold = far[:shard]
    keep = keep[: count // 4] + other.astype(F32)
    for a in ("z2",):
        half = keep.shape[0] // 2
        keep = keep[:half] + swap(keep[half:].astype(BF), a).astype(F32)
    grad_hot = spread(far[shard:], HALF).reshape(-1, width)
    grad_hot = spread(grad_hot, NEAR)
    grad_hot, keep = lax.optimization_barrier((grad_hot, keep))
    grad_hot = grad_hot.reshape(hot // 2, width)
    grad_hot = pl.pallas_call(
        place_kernel,
        out_shape=jax.ShapeDtypeStruct((hot, width), BF),
        in_specs=[smem, vmem, vmem],
        out_specs=pl.BlockSpec(memory_space=pl.ANY),
        scratch_shapes=[pltpu.SemaphoreType.DMA((2,))],
        compiler_params=params,
    )(at_me, grad_hot, swap(grad_hot, "c"))
    return keep.astype(BF), grad_hot, grad_cold, loss[0]


def solution(mesh):
    fine = Mesh(mesh.devices.reshape((2,) * len(AXES)), AXES)
    rows = P(AXES, None)
    return jax.shard_map(
        body,
        mesh=fine,
        in_specs=(rows, P(), rows, P(), P()),
        out_specs=(rows, P(), rows, P(AXES)),
        check_vma=False,
    )
```

```python
import functools

import jax
import jax.numpy as jnp
from jax import lax
from jax.experimental import pallas as pl
from jax.experimental.pallas import tpu as pltpu
from jax.sharding import Mesh
from jax.sharding import PartitionSpec as P

AXES = ("z8", "z4", "z2", "z1", "yl", "c", "x2", "x1", "yh")
COLS = ("c", "z2", "z1")
HALF = ("z2", "z1")
NEAR = ("yl", "x2", "x1", "yh")
FAR = ("z8", "z4")
NC, NG, NF = 2 ** len(COLS), 2 ** len(NEAR), 2 ** len(FAR)
BF = jnp.bfloat16
F32 = jnp.float32
NT = (((1,), (1,)), ((), ()))
TN = (((0,), (0,)), ((), ()))
CHUNKS = 4


def spread(x, axes):
    n = lax.axis_size(axes)
    return lax.all_to_all(jnp.broadcast_to(x[None], (n, *x.shape)), axes, 0, 0)


def swap(x, axis):
    return lax.ppermute(x, axis, [(0, 1), (1, 0)])


def bit(index, axis):
    return (index >> (len(AXES) - 1 - AXES.index(axis))) & 1


def pick(index, axes):
    out = 0
    for a in axes:
        out = out * 2 + bit(index, a)
    return out


def flip(p):
    mask = 0
    for a in reversed(COLS):
        mask |= (p & 1) << (len(AXES) - 1 - AXES.index(a))
        p >>= 1
    return mask


def decode_kernel(me_ref, ids_ref, targets_ref, out_ref, aim_ref, sems):
    me = me_ref[0]
    k = pick(me, COLS)
    groups, lanes = ids_ref.shape
    copies = []
    for p in range(NC):
        here = aim_ref.at[:, pl.ds(p * lanes, lanes)]
        copies.append(pltpu.make_async_copy(targets_ref.at[me ^ flip(p)], here, sems.at[p]))
        copies[p].start()
    hot_own = groups * lanes // (NC * NG)
    shard = 32
    near_chunk = NG // CHUNKS
    width = near_chunk * (NF * shard + hot_own)
    for copy in copies:
        copy.wait()
    aim = aim_ref[...]
    below = jnp.zeros(aim.shape, jnp.int32)
    slot = jnp.zeros(aim.shape, jnp.int32)
    for i in range(groups):
        ids = jnp.broadcast_to(ids_ref[i : i + 1], (lanes, lanes)).T
        ids = jnp.concatenate([ids] * NC, axis=1)
        place = lax.broadcasted_iota(jnp.int32, ids.shape, 0) + (i * lanes + 1)
        below += jnp.sum((ids < aim).astype(jnp.int32), axis=0, keepdims=True)
        slot += jnp.sum(jnp.where(ids == aim, place, 0), axis=0, keepdims=True)
    slot -= 1
    is_hot = slot >= 0
    row = aim - below
    block = row >> 5
    near = pick(block, NEAR)
    cold_col = near // near_chunk * width + (near % near_chunk) * (NF * shard)
    cold_col += pick(block, FAR) * shard + (row & (shard - 1))
    hot_near = (slot >> 6) & (NG - 1)
    hot_k = ((slot >> 10) << 2) | ((slot >> 4) & 3)
    hot_col = hot_near // near_chunk * width + near_chunk * NF * shard
    hot_col += (hot_near % near_chunk) * hot_own + (slot & (hot_own - 1))
    column = jnp.where(is_hot, hot_col, cold_col)
    there = jnp.where(is_hot, hot_k, pick(block, COLS))
    out_ref[...] = jnp.where(there == k, column, -1)


def chunk_table(cold_ref, hot_ref, g):
    n = NG // CHUNKS
    cold = cold_ref[pl.ds(g * n, n)]
    hot = hot_ref[pl.ds(g * n, n)]
    wide = cold.shape[-1]
    return jnp.concatenate([cold.reshape(-1, wide), hot.reshape(-1, wide)], axis=0)


def stats_kernel(me_ref, cold_ref, hot_ref, col_ref, *refs):
    *row_refs, out_ref = refs
    rows = jnp.concatenate([r[...] for r in row_refs], axis=0)
    cols = col_ref[...]
    count = rows.shape[0]
    k = pick(me_ref[0], COLS)

    def step(g, carry):
        top, total, hit = carry
        table = chunk_table(cold_ref, hot_ref, g)
        s = lax.dot_general(table, rows, NT, preferred_element_type=F32)
        new = jnp.maximum(top, jnp.max(s, axis=0, keepdims=True))
        total = total * jnp.exp(top - new) + jnp.sum(jnp.exp(s - new), axis=0, keepdims=True)
        where = lax.broadcasted_iota(jnp.int32, s.shape, 0) == cols - g * table.shape[0]
        hit = hit + jnp.sum(jnp.where(where, s, 0.0), axis=0, keepdims=True)
        return new, total, hit

    zero = jnp.zeros((1, count), F32)
    start = (jnp.full((1, count), -1e30, F32), zero, zero)
    top, total, hit = lax.fori_loop(0, CHUNKS, step, start, unroll=True)
    logs = top + jnp.log(total)
    for p in range(NC):
        here = slice(p * 128, (p + 1) * 128)
        there = pl.ds(pl.multiple_of((k ^ p) * 128, 128), 128)
        for d in range(NC):
            out_ref[d, 0:1, there] = logs[:, here]
            out_ref[d, 1:2, there] = hit[:, here]


def grads_kernel(me_ref, cold_ref, hot_ref, col_ref, stats_ref, *refs):
    *row_refs, keep_ref, send_ref, item_ref, loss_ref, acc_ref = refs
    rows = jnp.concatenate([r[...] for r in row_refs], axis=0)
    cols = col_ref[...]
    k = pick(me_ref[0], COLS)
    pieces = []
    for p in range(NC):
        there = pl.ds(pl.multiple_of((k ^ p) * 128, 128), 128)
        tops = [stats_ref[d, 0:1, there] for d in range(NC)]
        top = functools.reduce(jnp.maximum, tops)
        total = sum(jnp.exp(t - top) for t in tops)
        pieces.append(top + jnp.log(total))
        if p == 0:
            loss_ref[...] = pieces[0] - sum(stats_ref[d, 1:2, there] for d in range(NC))
    logs = jnp.concatenate(pieces, axis=1)
    acc_ref[...] = jnp.zeros_like(acc_ref)
    n = NG // CHUNKS
    cold_rows = cold_ref.shape[1]

    def step(g, carry):
        table = chunk_table(cold_ref, hot_ref, g)
        s = lax.dot_general(table, rows, NT, preferred_element_type=F32)
        where = lax.broadcasted_iota(jnp.int32, s.shape, 0) == cols - g * table.shape[0]
        w = (jnp.exp(s - logs) - jnp.where(where, 1.0, 0.0)).astype(BF)
        item = jnp.dot(w, rows, preferred_element_type=F32).astype(BF)
        wide = item.shape[-1]
        item_ref[pl.ds(g * n, n), :cold_rows] = item[: n * cold_rows].reshape(n, -1, wide)
        item_ref[pl.ds(g * n, n), cold_rows:] = item[n * cold_rows :].reshape(n, -1, wide)
        acc_ref[...] += lax.dot_general(table, w, TN, preferred_element_type=F32)
        return carry

    lax.fori_loop(0, CHUNKS, step, 0, unroll=True)
    half = acc_ref.shape[1] // 2
    keep_ref[...] = acc_ref[:, :half].T
    send_ref[...] = acc_ref[:, half:].T.astype(BF)


def place_kernel(me_ref, own_ref, other_ref, out_ref, sems):
    core = bit(me_ref[0], "c")
    half = own_ref.shape[0]
    first = pltpu.make_async_copy(own_ref, out_ref.at[pl.ds(core * half, half)], sems.at[0])
    second = pltpu.make_async_copy(
        other_ref, out_ref.at[pl.ds((1 - core) * half, half)], sems.at[1]
    )
    first.start()
    second.start()
    first.wait()
    second.wait()


def body(queries, hot_table, cold_table, hot_ids, targets):
    own, width = queries.shape
    shard = cold_table.shape[0]
    hot = hot_table.shape[0]
    hot_own = hot // (NC * NG)
    me = lax.axis_index(AXES)
    at_me = jnp.reshape(me, (1,)).astype(jnp.int32)
    k = pick(me, COLS)
    count = NC * own
    params = pltpu.CompilerParams(vmem_limit_bytes=24 << 20)
    vmem = pl.BlockSpec(memory_space=pltpu.VMEM)
    smem = pl.BlockSpec(memory_space=pltpu.SMEM)

    rows = [queries, swap(queries, "z1")]
    late_me, rows[1] = lax.optimization_barrier((at_me, rows[1]))

    column = pl.pallas_call(
        decode_kernel,
        out_shape=jax.ShapeDtypeStruct((1, count), jnp.int32),
        in_specs=[smem, vmem, pl.BlockSpec(memory_space=pltpu.HBM)],
        scratch_shapes=[pltpu.VMEM((1, count), jnp.int32), pltpu.SemaphoreType.DMA((NC,))],
        cost_estimate=pl.CostEstimate(
            flops=hot * count << 11, bytes_accessed=1 << 20, transcendentals=0
        ),
        compiler_params=params,
    )(late_me, hot_ids.reshape(-1, 128), targets.reshape(-1, 1, own))

    far = spread(cold_table, FAR).reshape(NF * shard, width)
    far, column = lax.optimization_barrier((far, column))
    cold = spread(far, NEAR)
    for a in ("z2", "c"):
        rows.append(swap(jnp.concatenate(rows, axis=0), a))
    mine = hot_table.reshape(2, NG, NC // 2, hot_own, width)
    mine = lax.dynamic_slice(mine, (k >> 2, 0, k & 3, 0, 0), (1, NG, 1, hot_own, width))
    mine = mine.reshape(NG, hot_own, width)

    stats = pl.pallas_call(
        stats_kernel,
        out_shape=jax.ShapeDtypeStruct((NC, 2, count), F32),
        in_specs=[smem] + [vmem] * (3 + len(rows)),
        compiler_params=params,
    )(at_me, cold, mine, column, *rows)
    stats = lax.all_to_all(stats, COLS, 0, 0)
    keep, send, item_part, loss = pl.pallas_call(
        grads_kernel,
        out_shape=(
            jax.ShapeDtypeStruct((count // 2, width), F32),
            jax.ShapeDtypeStruct((count // 2, width), BF),
            jax.ShapeDtypeStruct((NG, NF * shard + hot_own, width), BF),
            jax.ShapeDtypeStruct((1, own), F32),
        ),
        in_specs=[smem] + [vmem] * (4 + len(rows)),
        scratch_shapes=[pltpu.VMEM((width, count), F32)],
        compiler_params=params,
    )(at_me, cold, mine, column, stats, *rows)

    near = lax.all_to_all(item_part, NEAR, 0, 0)
    keep = keep + swap(send, "c").astype(F32)
    other = swap(keep[count // 4 :].astype(BF), "z2")
    near, other = lax.optimization_barrier((near, other))
    keep = keep[: count // 4] + other.astype(F32)
    near = jnp.sum(near.astype(F32), axis=0).astype(BF)
    cold_part = near[: NF * shard].reshape(NF, shard, width)
    hot_part = jnp.broadcast_to(near[None, NF * shard :], (NF, hot_own, width))
    far = lax.all_to_all(jnp.concatenate([cold_part, hot_part], axis=1), FAR, 0, 0)
    other = swap(keep[own:].astype(BF), "z1")
    far, other = lax.optimization_barrier((far, other))
    grad_queries = (keep[:own] + other.astype(F32)).astype(BF)
    far = jnp.sum(far.astype(F32), axis=0).astype(BF)
    grad_cold = far[:shard]
    grad_hot = spread(far[shard:], HALF).reshape(-1, width)
    grad_hot = spread(grad_hot, NEAR)
    grad_hot, grad_queries = lax.optimization_barrier((grad_hot, grad_queries))
    grad_hot = grad_hot.reshape(hot // 2, width)
    grad_hot = pl.pallas_call(
        place_kernel,
        out_shape=jax.ShapeDtypeStruct((hot, width), BF),
        in_specs=[smem, vmem, vmem],
        out_specs=pl.BlockSpec(memory_space=pl.ANY),
        scratch_shapes=[pltpu.SemaphoreType.DMA((2,))],
        compiler_params=params,
    )(at_me, grad_hot, swap(grad_hot, "c"))
    return grad_queries, grad_hot, grad_cold, loss[0]


def solution(mesh):
    fine = Mesh(mesh.devices.reshape((2,) * len(AXES)), AXES)
    rows = P(AXES, None)
    return jax.shard_map(
        body,
        mesh=fine,
        in_specs=(rows, P(), rows, P(), P()),
        out_specs=(rows, P(), rows, P(AXES)),
        check_vma=False,
    )
```

```python
import functools

import jax
import jax.numpy as jnp
from jax import lax
from jax.experimental import pallas as pl
from jax.experimental.pallas import tpu as pltpu
from jax.sharding import Mesh
from jax.sharding import PartitionSpec as P

AXES = ("z8", "z4", "z2", "z1", "yl", "c", "x2", "x1", "yh")
COLS = ("c", "z2", "z1")
HALF = ("z2", "z1")
NEAR = ("yl", "x2", "x1", "yh")
FAR = ("z8", "z4")
NC, NG, NF = 2 ** len(COLS), 2 ** len(NEAR), 2 ** len(FAR)
BF = jnp.bfloat16
F32 = jnp.float32
NT = (((1,), (1,)), ((), ()))
TN = (((0,), (0,)), ((), ()))
CHUNKS = 4


def spread(x, axes):
    n = lax.axis_size(axes)
    return lax.all_to_all(jnp.broadcast_to(x[None], (n, *x.shape)), axes, 0, 0)


def swap(x, axis):
    return lax.ppermute(x, axis, [(0, 1), (1, 0)])


def bit(index, axis):
    return (index >> (len(AXES) - 1 - AXES.index(axis))) & 1


def pick(index, axes):
    out = 0
    for a in axes:
        out = out * 2 + bit(index, a)
    return out


def flip(p):
    mask = 0
    for a in reversed(COLS):
        mask |= (p & 1) << (len(AXES) - 1 - AXES.index(a))
        p >>= 1
    return mask


def decode_kernel(me_ref, ids_ref, targets_ref, out_ref, aim_ref, sems):
    me = me_ref[0]
    k = pick(me, COLS)
    groups, lanes = ids_ref.shape
    copies = []
    for p in range(NC):
        here = aim_ref.at[:, pl.ds(p * lanes, lanes)]
        copies.append(pltpu.make_async_copy(targets_ref.at[me ^ flip(p)], here, sems.at[p]))
        copies[p].start()
    hot_own = groups * lanes // (NC * NG)
    shard = 32
    near_chunk = NG // CHUNKS
    width = near_chunk * (NF * shard + hot_own)
    for copy in copies:
        copy.wait()
    aim = aim_ref[...]
    below = jnp.zeros(aim.shape, jnp.int32)
    slot = jnp.zeros(aim.shape, jnp.int32)
    for i in range(groups):
        ids = jnp.broadcast_to(ids_ref[i : i + 1], (lanes, lanes)).T
        ids = jnp.concatenate([ids] * NC, axis=1)
        place = lax.broadcasted_iota(jnp.int32, ids.shape, 0) + (i * lanes + 1)
        below += jnp.sum((ids < aim).astype(jnp.int32), axis=0, keepdims=True)
        slot += jnp.sum(jnp.where(ids == aim, place, 0), axis=0, keepdims=True)
    slot -= 1
    is_hot = slot >= 0
    row = aim - below
    block = row >> 5
    near = pick(block, NEAR)
    cold_col = near // near_chunk * width + (near % near_chunk) * (NF * shard)
    cold_col += pick(block, FAR) * shard + (row & (shard - 1))
    hot_near = (slot >> 6) & (NG - 1)
    hot_k = ((slot >> 10) << 2) | ((slot >> 4) & 3)
    hot_col = hot_near // near_chunk * width + near_chunk * NF * shard
    hot_col += (hot_near % near_chunk) * hot_own + (slot & (hot_own - 1))
    column = jnp.where(is_hot, hot_col, cold_col)
    there = jnp.where(is_hot, hot_k, pick(block, COLS))
    out_ref[...] = jnp.where(there == k, column, -1)


def chunk_table(cold_ref, hot_ref, g):
    n = NG // CHUNKS
    cold = cold_ref[pl.ds(g * n, n)]
    hot = hot_ref[pl.ds(g * n, n)]
    wide = cold.shape[-1]
    return jnp.concatenate([cold.reshape(-1, wide), hot.reshape(-1, wide)], axis=0)


def stats_kernel(me_ref, cold_ref, hot_ref, col_ref, *refs):
    *row_refs, out_ref = refs
    rows = jnp.concatenate([r[...] for r in row_refs], axis=0)
    cols = col_ref[...]
    count = rows.shape[0]
    k = pick(me_ref[0], COLS)

    def step(g, carry):
        top, total, hit = carry
        table = chunk_table(cold_ref, hot_ref, g)
        s = lax.dot_general(table, rows, NT, preferred_element_type=F32)
        new = jnp.maximum(top, jnp.max(s, axis=0, keepdims=True))
        total = total * jnp.exp(top - new) + jnp.sum(jnp.exp(s - new), axis=0, keepdims=True)
        where = lax.broadcasted_iota(jnp.int32, s.shape, 0) == cols - g * table.shape[0]
        hit = hit + jnp.sum(jnp.where(where, s, 0.0), axis=0, keepdims=True)
        return new, total, hit

    zero = jnp.zeros((1, count), F32)
    start = (jnp.full((1, count), -1e30, F32), zero, zero)
    top, total, hit = lax.fori_loop(0, CHUNKS, step, start, unroll=True)
    logs = top + jnp.log(total)
    for p in range(NC):
        here = slice(p * 128, (p + 1) * 128)
        there = pl.ds(pl.multiple_of((k ^ p) * 128, 128), 128)
        for d in range(NC):
            out_ref[d, 0:1, there] = logs[:, here]
            out_ref[d, 1:2, there] = hit[:, here]


def grads_kernel(me_ref, cold_ref, hot_ref, col_ref, stats_ref, *refs):
    *row_refs, keep_ref, send_ref, item_ref, loss_ref, acc_ref = refs
    rows = jnp.concatenate([r[...] for r in row_refs], axis=0)
    cols = col_ref[...]
    k = pick(me_ref[0], COLS)
    pieces = []
    for p in range(NC):
        there = pl.ds(pl.multiple_of((k ^ p) * 128, 128), 128)
        tops = [stats_ref[d, 0:1, there] for d in range(NC)]
        top = functools.reduce(jnp.maximum, tops)
        total = sum(jnp.exp(t - top) for t in tops)
        pieces.append(top + jnp.log(total))
        if p == 0:
            loss_ref[...] = pieces[0] - sum(stats_ref[d, 1:2, there] for d in range(NC))
    logs = jnp.concatenate(pieces, axis=1)
    acc_ref[...] = jnp.zeros_like(acc_ref)
    n = NG // CHUNKS
    cold_rows = cold_ref.shape[1]

    def step(g, carry):
        table = chunk_table(cold_ref, hot_ref, g)
        s = lax.dot_general(table, rows, NT, preferred_element_type=F32)
        where = lax.broadcasted_iota(jnp.int32, s.shape, 0) == cols - g * table.shape[0]
        w = (jnp.exp(s - logs) - jnp.where(where, 1.0, 0.0)).astype(BF)
        item = jnp.dot(w, rows, preferred_element_type=F32).astype(BF)
        wide = item.shape[-1]
        item_ref[pl.ds(g * n, n), :cold_rows] = item[: n * cold_rows].reshape(n, -1, wide)
        item_ref[pl.ds(g * n, n), cold_rows:] = item[n * cold_rows :].reshape(n, -1, wide)
        acc_ref[...] += lax.dot_general(table, w, TN, preferred_element_type=F32)
        return carry

    lax.fori_loop(0, CHUNKS, step, 0, unroll=True)
    half = acc_ref.shape[1] // 2
    keep_ref[...] = acc_ref[:, :half].T
    send_ref[...] = acc_ref[:, half:].T.astype(BF)


def place_kernel(me_ref, own_ref, other_ref, out_ref, sems):
    core = bit(me_ref[0], "c")
    half = own_ref.shape[0]
    first = pltpu.make_async_copy(own_ref, out_ref.at[pl.ds(core * half, half)], sems.at[0])
    second = pltpu.make_async_copy(
        other_ref, out_ref.at[pl.ds((1 - core) * half, half)], sems.at[1]
    )
    first.start()
    second.start()
    first.wait()
    second.wait()


def body(queries, hot_table, cold_table, hot_ids, targets):
    own, width = queries.shape
    shard = cold_table.shape[0]
    hot = hot_table.shape[0]
    hot_own = hot // (NC * NG)
    me = lax.axis_index(AXES)
    at_me = jnp.reshape(me, (1,)).astype(jnp.int32)
    k = pick(me, COLS)
    count = NC * own
    params = pltpu.CompilerParams(vmem_limit_bytes=24 << 20)
    vmem = pl.BlockSpec(memory_space=pltpu.VMEM)
    smem = pl.BlockSpec(memory_space=pltpu.SMEM)

    rows = [queries, swap(queries, "z1")]

    column = pl.pallas_call(
        decode_kernel,
        out_shape=jax.ShapeDtypeStruct((1, count), jnp.int32),
        in_specs=[smem, vmem, pl.BlockSpec(memory_space=pltpu.HBM)],
        scratch_shapes=[pltpu.VMEM((1, count), jnp.int32), pltpu.SemaphoreType.DMA((NC,))],
        cost_estimate=pl.CostEstimate(
            flops=6 * hot * count, bytes_accessed=1 << 20, transcendentals=0
        ),
        compiler_params=params,
    )(at_me, hot_ids.reshape(-1, 128), targets.reshape(-1, 1, own))

    far = spread(cold_table, FAR).reshape(NF * shard, width)
    far, rows[1] = lax.optimization_barrier((far, rows[1]))
    cold = spread(far, NEAR)
    rows = jnp.concatenate(rows, axis=0)
    other, column = lax.optimization_barrier((swap(rows, "z2"), column))
    rows = jnp.concatenate([rows, other], axis=0)
    rows = [rows, swap(rows, "c")]
    mine = hot_table.reshape(2, NG, NC // 2, hot_own, width)
    mine = lax.dynamic_slice(mine, (k >> 2, 0, k & 3, 0, 0), (1, NG, 1, hot_own, width))
    mine = mine.reshape(NG, hot_own, width)

    stats = pl.pallas_call(
        stats_kernel,
        out_shape=jax.ShapeDtypeStruct((NC, 2, count), F32),
        in_specs=[smem] + [vmem] * (3 + len(rows)),
        compiler_params=params,
    )(at_me, cold, mine, column, *rows)
    stats = lax.all_to_all(stats, COLS, 0, 0)
    keep, send, item_part, loss = pl.pallas_call(
        grads_kernel,
        out_shape=(
            jax.ShapeDtypeStruct((count // 2, width), F32),
            jax.ShapeDtypeStruct((count // 2, width), BF),
            jax.ShapeDtypeStruct((NG, NF * shard + hot_own, width), BF),
            jax.ShapeDtypeStruct((1, own), F32),
        ),
        in_specs=[smem] + [vmem] * (4 + len(rows)),
        scratch_shapes=[pltpu.VMEM((width, count), F32)],
        compiler_params=params,
    )(at_me, cold, mine, column, stats, *rows)

    near = lax.all_to_all(item_part, NEAR, 0, 0)
    keep = (keep + swap(send, "c").astype(F32)).reshape(4, own, width)
    sends = keep.astype(BF)
    others = [swap(sends[1], "z1"), swap(sends[2], "z2")]
    others.append(lax.ppermute(sends[3], ("z2", "z1"), [(i, 3 - i) for i in range(4)]))
    near, *others = lax.optimization_barrier((near, *others))
    grad_queries = (keep[0] + sum(x.astype(F32) for x in others)).astype(BF)
    near = jnp.sum(near.astype(F32), axis=0).astype(BF)
    cold_part = near[: NF * shard].reshape(NF, shard, width)
    hot_part = jnp.broadcast_to(near[None, NF * shard :], (NF, hot_own, width))
    far = lax.all_to_all(jnp.concatenate([cold_part, hot_part], axis=1), FAR, 0, 0)
    far = jnp.sum(far.astype(F32), axis=0).astype(BF)
    grad_cold = far[:shard]
    grad_hot = spread(far[shard:], HALF).reshape(-1, width)
    grad_hot = spread(grad_hot, NEAR)
    grad_hot = grad_hot.reshape(hot // 2, width)
    grad_hot = pl.pallas_call(
        place_kernel,
        out_shape=jax.ShapeDtypeStruct((hot, width), BF),
        in_specs=[smem, vmem, vmem],
        out_specs=pl.BlockSpec(memory_space=pl.ANY),
        scratch_shapes=[pltpu.SemaphoreType.DMA((2,))],
        compiler_params=params,
    )(at_me, grad_hot, swap(grad_hot, "c"))
    return grad_queries, grad_hot, grad_cold, loss[0]


def solution(mesh):
    fine = Mesh(mesh.devices.reshape((2,) * len(AXES)), AXES)
    rows = P(AXES, None)
    return jax.shard_map(
        body,
        mesh=fine,
        in_specs=(rows, P(), rows, P(), P()),
        out_specs=(rows, P(), rows, P(AXES)),
        check_vma=False,
    )
```

```python
import functools

import jax
import jax.numpy as jnp
from jax import lax
from jax.experimental import pallas as pl
from jax.experimental.pallas import tpu as pltpu
from jax.sharding import Mesh
from jax.sharding import PartitionSpec as P

AXES = ("z8", "z4", "z2", "z1", "yl", "c", "x2", "x1", "yh")
COLS = ("c", "z2", "z1")
HALF = ("z2", "z1")
NEAR = ("yl", "x2", "x1", "yh")
FAR = ("z8", "z4")
NC, NG, NF = 2 ** len(COLS), 2 ** len(NEAR), 2 ** len(FAR)
BF = jnp.bfloat16
F32 = jnp.float32
NT = (((1,), (1,)), ((), ()))
TN = (((0,), (0,)), ((), ()))
CHUNKS = 4


def spread(x, axes):
    n = lax.axis_size(axes)
    return lax.all_to_all(jnp.broadcast_to(x[None], (n, *x.shape)), axes, 0, 0)


def swap(x, axis):
    return lax.ppermute(x, axis, [(0, 1), (1, 0)])


def bit(index, axis):
    return (index >> (len(AXES) - 1 - AXES.index(axis))) & 1


def pick(index, axes):
    out = 0
    for a in axes:
        out = out * 2 + bit(index, a)
    return out


def flip(p):
    mask = 0
    for a in reversed(COLS):
        mask |= (p & 1) << (len(AXES) - 1 - AXES.index(a))
        p >>= 1
    return mask


def decode_kernel(me_ref, ids_ref, targets_ref, out_ref, aim_ref, sems):
    me = me_ref[0]
    k = pick(me, COLS)
    groups, lanes = ids_ref.shape
    copies = []
    for p in range(NC):
        here = aim_ref.at[:, pl.ds(p * lanes, lanes)]
        copies.append(pltpu.make_async_copy(targets_ref.at[me ^ flip(p)], here, sems.at[p]))
        copies[p].start()
    hot_own = groups * lanes // (NC * NG)
    shard = 32
    near_chunk = NG // CHUNKS
    width = near_chunk * (NF * shard + hot_own)
    for copy in copies:
        copy.wait()
    aim = aim_ref[...]
    below = jnp.zeros(aim.shape, jnp.int32)
    slot = jnp.zeros(aim.shape, jnp.int32)
    for i in range(groups):
        ids = jnp.broadcast_to(ids_ref[i : i + 1], (lanes, lanes)).T
        ids = jnp.concatenate([ids] * NC, axis=1)
        place = lax.broadcasted_iota(jnp.int32, ids.shape, 0) + (i * lanes + 1)
        below += jnp.sum((ids < aim).astype(jnp.int32), axis=0, keepdims=True)
        slot += jnp.sum(jnp.where(ids == aim, place, 0), axis=0, keepdims=True)
    slot -= 1
    is_hot = slot >= 0
    row = aim - below
    block = row >> 5
    near = pick(block, NEAR)
    cold_col = near // near_chunk * width + (near % near_chunk) * (NF * shard)
    cold_col += pick(block, FAR) * shard + (row & (shard - 1))
    hot_near = (slot >> 6) & (NG - 1)
    hot_k = ((slot >> 10) << 2) | ((slot >> 4) & 3)
    hot_col = hot_near // near_chunk * width + near_chunk * NF * shard
    hot_col += (hot_near % near_chunk) * hot_own + (slot & (hot_own - 1))
    column = jnp.where(is_hot, hot_col, cold_col)
    there = jnp.where(is_hot, hot_k, pick(block, COLS))
    out_ref[...] = jnp.where(there == k, column, -1)


def chunk_table(cold_ref, hot_ref, g):
    n = NG // CHUNKS
    cold = cold_ref[pl.ds(g * n, n)]
    hot = hot_ref[pl.ds(g * n, n)]
    wide = cold.shape[-1]
    return jnp.concatenate([cold.reshape(-1, wide), hot.reshape(-1, wide)], axis=0)


def stats_kernel(me_ref, cold_ref, hot_ref, col_ref, *refs):
    *row_refs, out_ref = refs
    rows = jnp.concatenate([r[...] for r in row_refs], axis=0)
    cols = col_ref[...]
    count = rows.shape[0]
    k = pick(me_ref[0], COLS)

    def step(g, carry):
        top, total, hit = carry
        table = chunk_table(cold_ref, hot_ref, g)
        s = lax.dot_general(table, rows, NT, preferred_element_type=F32)
        new = jnp.maximum(top, jnp.max(s, axis=0, keepdims=True))
        total = total * jnp.exp(top - new) + jnp.sum(jnp.exp(s - new), axis=0, keepdims=True)
        where = lax.broadcasted_iota(jnp.int32, s.shape, 0) == cols - g * table.shape[0]
        hit = hit + jnp.sum(jnp.where(where, s, 0.0), axis=0, keepdims=True)
        return new, total, hit

    zero = jnp.zeros((1, count), F32)
    start = (jnp.full((1, count), -1e30, F32), zero, zero)
    top, total, hit = lax.fori_loop(0, CHUNKS, step, start, unroll=True)
    logs = top + jnp.log(total)
    for p in range(NC):
        here = slice(p * 128, (p + 1) * 128)
        there = pl.ds(pl.multiple_of((k ^ p) * 128, 128), 128)
        for d in range(NC):
            out_ref[d, 0:1, there] = logs[:, here]
            out_ref[d, 1:2, there] = hit[:, here]


def grads_kernel(me_ref, cold_ref, hot_ref, col_ref, stats_ref, *refs):
    *row_refs, keep_ref, send_ref, item_ref, loss_ref, acc_ref = refs
    rows = jnp.concatenate([r[...] for r in row_refs], axis=0)
    cols = col_ref[...]
    k = pick(me_ref[0], COLS)
    pieces = []
    for p in range(NC):
        there = pl.ds(pl.multiple_of((k ^ p) * 128, 128), 128)
        tops = [stats_ref[d, 0:1, there] for d in range(NC)]
        top = functools.reduce(jnp.maximum, tops)
        total = sum(jnp.exp(t - top) for t in tops)
        pieces.append(top + jnp.log(total))
        if p == 0:
            loss_ref[...] = pieces[0] - sum(stats_ref[d, 1:2, there] for d in range(NC))
    logs = jnp.concatenate(pieces, axis=1)
    acc_ref[...] = jnp.zeros_like(acc_ref)
    n = NG // CHUNKS
    cold_rows = cold_ref.shape[1]

    def step(g, carry):
        table = chunk_table(cold_ref, hot_ref, g)
        s = lax.dot_general(table, rows, NT, preferred_element_type=F32)
        where = lax.broadcasted_iota(jnp.int32, s.shape, 0) == cols - g * table.shape[0]
        w = (jnp.exp(s - logs) - jnp.where(where, 1.0, 0.0)).astype(BF)
        item = jnp.dot(w, rows, preferred_element_type=F32).astype(BF)
        wide = item.shape[-1]
        item_ref[pl.ds(g * n, n), :cold_rows] = item[: n * cold_rows].reshape(n, -1, wide)
        item_ref[pl.ds(g * n, n), cold_rows:] = item[n * cold_rows :].reshape(n, -1, wide)
        acc_ref[...] += lax.dot_general(table, w, TN, preferred_element_type=F32)
        return carry

    lax.fori_loop(0, CHUNKS, step, 0, unroll=True)
    half = acc_ref.shape[1] // 2
    keep_ref[...] = acc_ref[:, :half].T
    send_ref[...] = acc_ref[:, half:].T.astype(BF)


def place_kernel(me_ref, own_ref, other_ref, out_ref, sems):
    core = bit(me_ref[0], "c")
    half = own_ref.shape[0]
    first = pltpu.make_async_copy(own_ref, out_ref.at[pl.ds(core * half, half)], sems.at[0])
    second = pltpu.make_async_copy(
        other_ref, out_ref.at[pl.ds((1 - core) * half, half)], sems.at[1]
    )
    first.start()
    second.start()
    first.wait()
    second.wait()


def body(queries, hot_table, cold_table, hot_ids, targets):
    own, width = queries.shape
    shard = cold_table.shape[0]
    hot = hot_table.shape[0]
    hot_own = hot // (NC * NG)
    me = lax.axis_index(AXES)
    at_me = jnp.reshape(me, (1,)).astype(jnp.int32)
    k = pick(me, COLS)
    count = NC * own
    params = pltpu.CompilerParams(vmem_limit_bytes=24 << 20)
    vmem = pl.BlockSpec(memory_space=pltpu.VMEM)
    smem = pl.BlockSpec(memory_space=pltpu.SMEM)

    rows = [queries, swap(queries, "z1")]

    column = pl.pallas_call(
        decode_kernel,
        out_shape=jax.ShapeDtypeStruct((1, count), jnp.int32),
        in_specs=[smem, vmem, pl.BlockSpec(memory_space=pltpu.HBM)],
        scratch_shapes=[pltpu.VMEM((1, count), jnp.int32), pltpu.SemaphoreType.DMA((NC,))],
        cost_estimate=pl.CostEstimate(
            flops=6 * hot * count, bytes_accessed=1 << 20, transcendentals=0
        ),
        compiler_params=params,
    )(at_me, hot_ids.reshape(-1, 128), targets.reshape(-1, 1, own))

    far = spread(cold_table, FAR).reshape(NF * shard, width)
    far, rows[1] = lax.optimization_barrier((far, rows[1]))
    cold = spread(far, NEAR)
    rows = jnp.concatenate(rows, axis=0)
    other, column = lax.optimization_barrier((swap(rows, "z2"), column))
    rows = jnp.concatenate([rows, other], axis=0)
    rows = [rows, swap(rows, "c")]
    mine = hot_table.reshape(2, NG, NC // 2, hot_own, width)
    mine = lax.dynamic_slice(mine, (k >> 2, 0, k & 3, 0, 0), (1, NG, 1, hot_own, width))
    mine = mine.reshape(NG, hot_own, width)

    stats = pl.pallas_call(
        stats_kernel,
        out_shape=jax.ShapeDtypeStruct((NC, 2, count), F32),
        in_specs=[smem] + [vmem] * (3 + len(rows)),
        compiler_params=params,
    )(at_me, cold, mine, column, *rows)
    stats = lax.all_to_all(stats, COLS, 0, 0)
    keep, send, item_part, loss = pl.pallas_call(
        grads_kernel,
        out_shape=(
            jax.ShapeDtypeStruct((count // 2, width), F32),
            jax.ShapeDtypeStruct((count // 2, width), BF),
            jax.ShapeDtypeStruct((NG, NF * shard + hot_own, width), BF),
            jax.ShapeDtypeStruct((1, own), F32),
        ),
        in_specs=[smem] + [vmem] * (4 + len(rows)),
        scratch_shapes=[pltpu.VMEM((width, count), F32)],
        compiler_params=params,
    )(at_me, cold, mine, column, stats, *rows)

    near = lax.all_to_all(item_part, NEAR, 0, 0)
    keep = (keep + swap(send, "c").astype(F32)).reshape(4, own, width)
    sends = keep.astype(BF)
    others = [swap(sends[1], "z1"), swap(sends[2], "z2")]
    others.append(lax.ppermute(sends[3], ("z2", "z1"), [(i, 3 - i) for i in range(4)]))
    near, others[0] = lax.optimization_barrier((near, others[0]))
    near = jnp.sum(near.astype(F32), axis=0).astype(BF)
    cold_part = near[: NF * shard].reshape(NF, shard, width)
    hot_part = jnp.broadcast_to(near[None, NF * shard :], (NF, hot_own, width))
    far = lax.all_to_all(jnp.concatenate([cold_part, hot_part], axis=1), FAR, 0, 0)
    far = jnp.sum(far.astype(F32), axis=0).astype(BF)
    grad_cold = far[:shard]
    grad_hot = spread(far[shard:], HALF).reshape(-1, width)
    grad_hot = spread(grad_hot, NEAR)
    grad_hot, *others = lax.optimization_barrier((grad_hot, *others))
    grad_queries = (keep[0] + sum(x.astype(F32) for x in others)).astype(BF)
    grad_hot = grad_hot.reshape(hot // 2, width)
    grad_hot = pl.pallas_call(
        place_kernel,
        out_shape=jax.ShapeDtypeStruct((hot, width), BF),
        in_specs=[smem, vmem, vmem],
        out_specs=pl.BlockSpec(memory_space=pl.ANY),
        scratch_shapes=[pltpu.SemaphoreType.DMA((2,))],
        compiler_params=params,
    )(at_me, grad_hot, swap(grad_hot, "c"))
    return grad_queries, grad_hot, grad_cold, loss[0]


def solution(mesh):
    fine = Mesh(mesh.devices.reshape((2,) * len(AXES)), AXES)
    rows = P(AXES, None)
    return jax.shard_map(
        body,
        mesh=fine,
        in_specs=(rows, P(), rows, P(), P()),
        out_specs=(rows, P(), rows, P(AXES)),
        check_vma=False,
    )
```

```python
import functools

import jax
import jax.numpy as jnp
from jax import lax
from jax.experimental import pallas as pl
from jax.experimental.pallas import tpu as pltpu
from jax.sharding import Mesh
from jax.sharding import PartitionSpec as P

AXES = ("z8", "z4", "z2", "z1", "yl", "c", "x2", "x1", "yh")
COLS = ("c", "z2", "z1")
HALF = ("z2", "z1")
NEAR = ("yl", "x2", "x1", "yh")
FAR = ("z8", "z4")
NC, NG, NF = 2 ** len(COLS), 2 ** len(NEAR), 2 ** len(FAR)
BF = jnp.bfloat16
F32 = jnp.float32
NT = (((1,), (1,)), ((), ()))
TN = (((0,), (0,)), ((), ()))
CHUNKS = 4


def spread(x, axes):
    n = lax.axis_size(axes)
    return lax.all_to_all(jnp.broadcast_to(x[None], (n, *x.shape)), axes, 0, 0)


def swap(x, axis):
    return lax.ppermute(x, axis, [(0, 1), (1, 0)])


def bit(index, axis):
    return (index >> (len(AXES) - 1 - AXES.index(axis))) & 1


def pick(index, axes):
    out = 0
    for a in axes:
        out = out * 2 + bit(index, a)
    return out


def flip(p):
    mask = 0
    for a in reversed(COLS):
        mask |= (p & 1) << (len(AXES) - 1 - AXES.index(a))
        p >>= 1
    return mask


def decode_kernel(me_ref, ids_ref, targets_ref, out_ref, aim_ref, sems):
    me = me_ref[0]
    k = pick(me, COLS)
    groups, lanes = ids_ref.shape
    copies = []
    for p in range(NC):
        here = aim_ref.at[:, pl.ds(p * lanes, lanes)]
        copies.append(pltpu.make_async_copy(targets_ref.at[me ^ flip(p)], here, sems.at[p]))
        copies[p].start()
    hot_own = groups * lanes // (NC * NG)
    shard = 32
    near_chunk = NG // CHUNKS
    width = near_chunk * (NF * shard + hot_own)
    for copy in copies:
        copy.wait()
    aim = aim_ref[...]
    below = jnp.zeros(aim.shape, jnp.int32)
    slot = jnp.zeros(aim.shape, jnp.int32)
    for i in range(groups):
        ids = jnp.broadcast_to(ids_ref[i : i + 1], (lanes, lanes)).T
        ids = jnp.concatenate([ids] * NC, axis=1)
        place = lax.broadcasted_iota(jnp.int32, ids.shape, 0) + (i * lanes + 1)
        below += jnp.sum((ids < aim).astype(jnp.int32), axis=0, keepdims=True)
        slot += jnp.sum(jnp.where(ids == aim, place, 0), axis=0, keepdims=True)
    slot -= 1
    is_hot = slot >= 0
    row = aim - below
    block = row >> 5
    near = pick(block, NEAR)
    cold_col = near // near_chunk * width + (near % near_chunk) * (NF * shard)
    cold_col += (pick(block, FAR) ^ pick(me, FAR)) * shard + (row & (shard - 1))
    hot_near = (slot >> 6) & (NG - 1)
    hot_k = ((slot >> 10) << 2) | ((slot >> 4) & 3)
    hot_col = hot_near // near_chunk * width + near_chunk * NF * shard
    hot_col += (hot_near % near_chunk) * hot_own + (slot & (hot_own - 1))
    column = jnp.where(is_hot, hot_col, cold_col)
    there = jnp.where(is_hot, hot_k, pick(block, COLS))
    out_ref[...] = jnp.where(there == k, column, -1)


def chunk_table(cold_ref, hot_ref, g):
    n = NG // CHUNKS
    cold = cold_ref[pl.ds(g * n, n)]
    hot = hot_ref[pl.ds(g * n, n)]
    wide = cold.shape[-1]
    return jnp.concatenate([cold.reshape(-1, wide), hot.reshape(-1, wide)], axis=0)


def stats_kernel(me_ref, cold_ref, hot_ref, col_ref, *refs):
    *row_refs, out_ref = refs
    rows = jnp.concatenate([r[...] for r in row_refs], axis=0)
    cols = col_ref[...]
    count = rows.shape[0]
    k = pick(me_ref[0], COLS)

    def step(g, carry):
        top, total, hit = carry
        table = chunk_table(cold_ref, hot_ref, g)
        s = lax.dot_general(table, rows, NT, preferred_element_type=F32)
        new = jnp.maximum(top, jnp.max(s, axis=0, keepdims=True))
        total = total * jnp.exp(top - new) + jnp.sum(jnp.exp(s - new), axis=0, keepdims=True)
        where = lax.broadcasted_iota(jnp.int32, s.shape, 0) == cols - g * table.shape[0]
        hit = hit + jnp.sum(jnp.where(where, s, 0.0), axis=0, keepdims=True)
        return new, total, hit

    zero = jnp.zeros((1, count), F32)
    start = (jnp.full((1, count), -1e30, F32), zero, zero)
    top, total, hit = lax.fori_loop(0, CHUNKS, step, start, unroll=True)
    logs = top + jnp.log(total)
    for p in range(NC):
        here = slice(p * 128, (p + 1) * 128)
        there = pl.ds(pl.multiple_of((k ^ p) * 128, 128), 128)
        for d in range(NC):
            out_ref[d, 0:1, there] = logs[:, here]
            out_ref[d, 1:2, there] = hit[:, here]


def grads_kernel(me_ref, cold_ref, hot_ref, col_ref, stats_ref, *refs):
    *row_refs, keep_ref, send_ref, item_ref, loss_ref, acc_ref = refs
    rows = jnp.concatenate([r[...] for r in row_refs], axis=0)
    cols = col_ref[...]
    k = pick(me_ref[0], COLS)
    pieces = []
    for p in range(NC):
        there = pl.ds(pl.multiple_of((k ^ p) * 128, 128), 128)
        tops = [stats_ref[d, 0:1, there] for d in range(NC)]
        top = functools.reduce(jnp.maximum, tops)
        total = sum(jnp.exp(t - top) for t in tops)
        pieces.append(top + jnp.log(total))
        if p == 0:
            loss_ref[...] = pieces[0] - sum(stats_ref[d, 1:2, there] for d in range(NC))
    logs = jnp.concatenate(pieces, axis=1)
    acc_ref[...] = jnp.zeros_like(acc_ref)
    n = NG // CHUNKS
    cold_rows = cold_ref.shape[1]
    shard = cold_rows // NF
    f = pick(me_ref[0], FAR)

    def step(g, carry):
        table = chunk_table(cold_ref, hot_ref, g)
        s = lax.dot_general(table, rows, NT, preferred_element_type=F32)
        where = lax.broadcasted_iota(jnp.int32, s.shape, 0) == cols - g * table.shape[0]
        w = (jnp.exp(s - logs) - jnp.where(where, 1.0, 0.0)).astype(BF)
        item = jnp.dot(w, rows, preferred_element_type=F32).astype(BF)
        wide = item.shape[-1]
        cold = item[: n * cold_rows].reshape(n, NF, shard, wide)
        for q in range(NF):
            there = pl.ds(pl.multiple_of((q ^ f) * shard, shard), shard)
            item_ref[pl.ds(g * n, n), there] = cold[:, q]
        item_ref[pl.ds(g * n, n), cold_rows:] = item[n * cold_rows :].reshape(n, -1, wide)
        acc_ref[...] += lax.dot_general(table, w, TN, preferred_element_type=F32)
        return carry

    lax.fori_loop(0, CHUNKS, step, 0, unroll=True)
    half = acc_ref.shape[1] // 2
    keep_ref[...] = acc_ref[:, :half].T
    send_ref[...] = acc_ref[:, half:].T.astype(BF)


def place_kernel(me_ref, own_ref, other_ref, out_ref, sems):
    core = bit(me_ref[0], "c")
    half = own_ref.shape[0]
    first = pltpu.make_async_copy(own_ref, out_ref.at[pl.ds(core * half, half)], sems.at[0])
    second = pltpu.make_async_copy(
        other_ref, out_ref.at[pl.ds((1 - core) * half, half)], sems.at[1]
    )
    first.start()
    second.start()
    first.wait()
    second.wait()


def body(queries, hot_table, cold_table, hot_ids, targets):
    own, width = queries.shape
    shard = cold_table.shape[0]
    hot = hot_table.shape[0]
    hot_own = hot // (NC * NG)
    me = lax.axis_index(AXES)
    at_me = jnp.reshape(me, (1,)).astype(jnp.int32)
    k = pick(me, COLS)
    count = NC * own
    params = pltpu.CompilerParams(vmem_limit_bytes=24 << 20)
    vmem = pl.BlockSpec(memory_space=pltpu.VMEM)
    smem = pl.BlockSpec(memory_space=pltpu.SMEM)

    rows = [queries, swap(queries, "z1")]

    column = pl.pallas_call(
        decode_kernel,
        out_shape=jax.ShapeDtypeStruct((1, count), jnp.int32),
        in_specs=[smem, vmem, pl.BlockSpec(memory_space=pltpu.HBM)],
        scratch_shapes=[pltpu.VMEM((1, count), jnp.int32), pltpu.SemaphoreType.DMA((NC,))],
        cost_estimate=pl.CostEstimate(
            flops=6 * hot * count, bytes_accessed=1 << 20, transcendentals=0
        ),
        compiler_params=params,
    )(at_me, hot_ids.reshape(-1, 128), targets.reshape(-1, 1, own))

    far = [cold_table, swap(cold_table, "z4"), swap(cold_table, "z8")]
    far.append(lax.ppermute(cold_table, ("z8", "z4"), [(i, 3 - i) for i in range(4)]))
    far, rows[1] = lax.optimization_barrier((jnp.concatenate(far, axis=0), rows[1]))
    cold = spread(far, NEAR)
    rows = jnp.concatenate(rows, axis=0)
    other, column = lax.optimization_barrier((swap(rows, "z2"), column))
    rows = jnp.concatenate([rows, other], axis=0)
    rows = [rows, swap(rows, "c")]
    mine = hot_table.reshape(2, NG, NC // 2, hot_own, width)
    mine = lax.dynamic_slice(mine, (k >> 2, 0, k & 3, 0, 0), (1, NG, 1, hot_own, width))
    mine = mine.reshape(NG, hot_own, width)

    stats = pl.pallas_call(
        stats_kernel,
        out_shape=jax.ShapeDtypeStruct((NC, 2, count), F32),
        in_specs=[smem] + [vmem] * (3 + len(rows)),
        compiler_params=params,
    )(at_me, cold, mine, column, *rows)
    stats = lax.all_to_all(stats, COLS, 0, 0)
    keep, send, item_part, loss = pl.pallas_call(
        grads_kernel,
        out_shape=(
            jax.ShapeDtypeStruct((count // 2, width), F32),
            jax.ShapeDtypeStruct((count // 2, width), BF),
            jax.ShapeDtypeStruct((NG, NF * shard + hot_own, width), BF),
            jax.ShapeDtypeStruct((1, own), F32),
        ),
        in_specs=[smem] + [vmem] * (4 + len(rows)),
        scratch_shapes=[pltpu.VMEM((width, count), F32)],
        compiler_params=params,
    )(at_me, cold, mine, column, stats, *rows)

    near = lax.all_to_all(item_part, NEAR, 0, 0)
    keep = (keep + swap(send, "c").astype(F32)).reshape(4, own, width)
    sends = keep.astype(BF)
    others = [swap(sends[1], "z1"), swap(sends[2], "z2")]
    others.append(lax.ppermute(sends[3], ("z2", "z1"), [(i, 3 - i) for i in range(4)]))
    near, *others = lax.optimization_barrier((near, *others))
    grad_queries = (keep[0] + sum(x.astype(F32) for x in others)).astype(BF)
    near = jnp.sum(near.astype(F32), axis=0).astype(BF)
    cold_part = near[: NF * shard].reshape(NF, shard, width)
    hot_part = jnp.broadcast_to(near[None, NF * shard :], (NF, hot_own, width))
    far = lax.all_to_all(jnp.concatenate([cold_part, hot_part], axis=1), FAR, 0, 0)
    far = jnp.sum(far.astype(F32), axis=0).astype(BF)
    grad_cold = far[:shard]
    grad_hot = spread(far[shard:], HALF).reshape(-1, width)
    grad_hot = spread(grad_hot, NEAR)
    grad_hot = grad_hot.reshape(hot // 2, width)
    grad_hot = pl.pallas_call(
        place_kernel,
        out_shape=jax.ShapeDtypeStruct((hot, width), BF),
        in_specs=[smem, vmem, vmem],
        out_specs=pl.BlockSpec(memory_space=pl.ANY),
        scratch_shapes=[pltpu.SemaphoreType.DMA((2,))],
        compiler_params=params,
    )(at_me, grad_hot, swap(grad_hot, "c"))
    return grad_queries, grad_hot, grad_cold, loss[0]


def solution(mesh):
    fine = Mesh(mesh.devices.reshape((2,) * len(AXES)), AXES)
    rows = P(AXES, None)
    return jax.shard_map(
        body,
        mesh=fine,
        in_specs=(rows, P(), rows, P(), P()),
        out_specs=(rows, P(), rows, P(AXES)),
        check_vma=False,
    )
```

```python
import functools

import jax
import jax.numpy as jnp
from jax import lax
from jax.experimental import pallas as pl
from jax.experimental.pallas import tpu as pltpu
from jax.sharding import Mesh
from jax.sharding import PartitionSpec as P

AXES = ("z8", "z4", "z2", "z1", "yl", "c", "x2", "x1", "yh")
COLS = ("c", "z2", "z1")
HALF = ("z2", "z1")
NEAR = ("x2", "x1", "yh", "yl")
FAR = ("z8", "z4")
NC, NG, NF = 2 ** len(COLS), 2 ** len(NEAR), 2 ** len(FAR)
BF = jnp.bfloat16
F32 = jnp.float32
NT = (((1,), (1,)), ((), ()))
TN = (((0,), (0,)), ((), ()))
CHUNKS = 4


def spread(x, axes):
    n = lax.axis_size(axes)
    return lax.all_to_all(jnp.broadcast_to(x[None], (n, *x.shape)), axes, 0, 0)


def swap(x, axis):
    return lax.ppermute(x, axis, [(0, 1), (1, 0)])


def bit(index, axis):
    return (index >> (len(AXES) - 1 - AXES.index(axis))) & 1


def pick(index, axes):
    out = 0
    for a in axes:
        out = out * 2 + bit(index, a)
    return out


def flip(p):
    mask = 0
    for a in reversed(COLS):
        mask |= (p & 1) << (len(AXES) - 1 - AXES.index(a))
        p >>= 1
    return mask


def decode_kernel(me_ref, ids_ref, targets_ref, out_ref, aim_ref, sems):
    me = me_ref[0]
    k = pick(me, COLS)
    groups, lanes = ids_ref.shape
    copies = []
    for p in range(NC):
        here = aim_ref.at[:, pl.ds(p * lanes, lanes)]
        copies.append(pltpu.make_async_copy(targets_ref.at[me ^ flip(p)], here, sems.at[p]))
        copies[p].start()
    hot_own = groups * lanes // (NC * NG)
    shard = 32
    near_chunk = NG // CHUNKS
    width = near_chunk * (NF * shard + hot_own)
    for copy in copies:
        copy.wait()
    aim = aim_ref[...]
    below = jnp.zeros(aim.shape, jnp.int32)
    slot = jnp.zeros(aim.shape, jnp.int32)
    for i in range(groups):
        ids = jnp.broadcast_to(ids_ref[i : i + 1], (lanes, lanes)).T
        ids = jnp.concatenate([ids] * NC, axis=1)
        place = lax.broadcasted_iota(jnp.int32, ids.shape, 0) + (i * lanes + 1)
        below += jnp.sum((ids < aim).astype(jnp.int32), axis=0, keepdims=True)
        slot += jnp.sum(jnp.where(ids == aim, place, 0), axis=0, keepdims=True)
    slot -= 1
    is_hot = slot >= 0
    row = aim - below
    block = row >> 5
    near = pick(block, NEAR)
    cold_col = near // near_chunk * width + (near % near_chunk) * (NF * shard)
    cold_col += pick(block, FAR) * shard + (row & (shard - 1))
    hot_near = (slot >> 6) & (NG - 1)
    hot_k = ((slot >> 10) << 2) | ((slot >> 4) & 3)
    hot_col = hot_near // near_chunk * width + near_chunk * NF * shard
    hot_col += (hot_near % near_chunk) * hot_own + (slot & (hot_own - 1))
    column = jnp.where(is_hot, hot_col, cold_col)
    there = jnp.where(is_hot, hot_k, pick(block, COLS))
    out_ref[...] = jnp.where(there == k, column, -1)


def chunk_table(cold_ref, hot_ref, g):
    n = NG // CHUNKS
    cold = cold_ref[pl.ds(g * n, n)]
    hot = hot_ref[pl.ds(g * n, n)]
    wide = cold.shape[-1]
    return jnp.concatenate([cold.reshape(-1, wide), hot.reshape(-1, wide)], axis=0)


def stats_kernel(me_ref, cold_ref, hot_ref, col_ref, *refs):
    *row_refs, out_ref = refs
    rows = jnp.concatenate([r[...] for r in row_refs], axis=0)
    cols = col_ref[...]
    count = rows.shape[0]
    k = pick(me_ref[0], COLS)

    def step(g, carry):
        top, total, hit = carry
        table = chunk_table(cold_ref, hot_ref, g)
        s = lax.dot_general(table, rows, NT, preferred_element_type=F32)
        new = jnp.maximum(top, jnp.max(s, axis=0, keepdims=True))
        total = total * jnp.exp(top - new) + jnp.sum(jnp.exp(s - new), axis=0, keepdims=True)
        where = lax.broadcasted_iota(jnp.int32, s.shape, 0) == cols - g * table.shape[0]
        hit = hit + jnp.sum(jnp.where(where, s, 0.0), axis=0, keepdims=True)
        return new, total, hit

    zero = jnp.zeros((1, count), F32)
    start = (jnp.full((1, count), -1e30, F32), zero, zero)
    top, total, hit = lax.fori_loop(0, CHUNKS, step, start, unroll=True)
    logs = top + jnp.log(total)
    for p in range(NC):
        here = slice(p * 128, (p + 1) * 128)
        there = pl.ds(pl.multiple_of((k ^ p) * 128, 128), 128)
        for d in range(NC):
            out_ref[d, 0:1, there] = logs[:, here]
            out_ref[d, 1:2, there] = hit[:, here]


def grads_kernel(me_ref, cold_ref, hot_ref, col_ref, stats_ref, *refs):
    *row_refs, keep_ref, send_ref, item_ref, loss_ref, acc_ref = refs
    rows = jnp.concatenate([r[...] for r in row_refs], axis=0)
    cols = col_ref[...]
    k = pick(me_ref[0], COLS)
    pieces = []
    for p in range(NC):
        there = pl.ds(pl.multiple_of((k ^ p) * 128, 128), 128)
        tops = [stats_ref[d, 0:1, there] for d in range(NC)]
        top = functools.reduce(jnp.maximum, tops)
        total = sum(jnp.exp(t - top) for t in tops)
        pieces.append(top + jnp.log(total))
        if p == 0:
            loss_ref[...] = pieces[0] - sum(stats_ref[d, 1:2, there] for d in range(NC))
    logs = jnp.concatenate(pieces, axis=1)
    acc_ref[...] = jnp.zeros_like(acc_ref)
    n = NG // CHUNKS
    cold_rows = cold_ref.shape[1]

    def step(g, carry):
        table = chunk_table(cold_ref, hot_ref, g)
        s = lax.dot_general(table, rows, NT, preferred_element_type=F32)
        where = lax.broadcasted_iota(jnp.int32, s.shape, 0) == cols - g * table.shape[0]
        w = (jnp.exp(s - logs) - jnp.where(where, 1.0, 0.0)).astype(BF)
        item = jnp.dot(w, rows, preferred_element_type=F32).astype(BF)
        wide = item.shape[-1]
        item_ref[pl.ds(g * n, n), :cold_rows] = item[: n * cold_rows].reshape(n, -1, wide)
        item_ref[pl.ds(g * n, n), cold_rows:] = item[n * cold_rows :].reshape(n, -1, wide)
        acc_ref[...] += lax.dot_general(table, w, TN, preferred_element_type=F32)
        return carry

    lax.fori_loop(0, CHUNKS, step, 0, unroll=True)
    half = acc_ref.shape[1] // 2
    keep_ref[...] = acc_ref[:, :half].T
    send_ref[...] = acc_ref[:, half:].T.astype(BF)


def place_kernel(first_ref, second_ref, out_ref, sems):
    part = first_ref.shape[1]
    copies = []
    for core in range(2):
        for i, ref in enumerate((first_ref, second_ref)):
            there = out_ref.at[pl.ds((2 * core + i) * part, part)]
            copies.append(pltpu.make_async_copy(ref.at[core], there, sems.at[2 * core + i]))
    for copy in copies:
        copy.start()
    for copy in copies:
        copy.wait()


def body(queries, hot_table, cold_table, hot_ids, targets):
    own, width = queries.shape
    shard = cold_table.shape[0]
    hot = hot_table.shape[0]
    hot_own = hot // (NC * NG)
    me = lax.axis_index(AXES)
    at_me = jnp.reshape(me, (1,)).astype(jnp.int32)
    k = pick(me, COLS)
    count = NC * own
    params = pltpu.CompilerParams(vmem_limit_bytes=24 << 20)
    vmem = pl.BlockSpec(memory_space=pltpu.VMEM)
    smem = pl.BlockSpec(memory_space=pltpu.SMEM)

    rows = [queries, swap(queries, "z1")]

    column = pl.pallas_call(
        decode_kernel,
        out_shape=jax.ShapeDtypeStruct((1, count), jnp.int32),
        in_specs=[smem, vmem, pl.BlockSpec(memory_space=pltpu.HBM)],
        scratch_shapes=[pltpu.VMEM((1, count), jnp.int32), pltpu.SemaphoreType.DMA((NC,))],
        cost_estimate=pl.CostEstimate(
            flops=6 * hot * count, bytes_accessed=1 << 20, transcendentals=0
        ),
        compiler_params=params,
    )(at_me, hot_ids.reshape(-1, 128), targets.reshape(-1, 1, own))

    far = spread(cold_table, FAR).reshape(NF * shard, width)
    far, rows[1] = lax.optimization_barrier((far, rows[1]))
    cold = spread(far, NEAR)
    rows = jnp.concatenate(rows, axis=0)
    other, column = lax.optimization_barrier((swap(rows, "z2"), column))
    rows = jnp.concatenate([rows, other], axis=0)
    rows = [rows, swap(rows, "c")]
    mine = hot_table.reshape(2, NG, NC // 2, hot_own, width)
    mine = lax.dynamic_slice(mine, (k >> 2, 0, k & 3, 0, 0), (1, NG, 1, hot_own, width))
    mine = mine.reshape(NG, hot_own, width)

    stats = pl.pallas_call(
        stats_kernel,
        out_shape=jax.ShapeDtypeStruct((NC, 2, count), F32),
        in_specs=[smem] + [vmem] * (3 + len(rows)),
        compiler_params=params,
    )(at_me, cold, mine, column, *rows)
    stats = lax.all_to_all(stats, COLS, 0, 0)
    keep, send, item_part, loss = pl.pallas_call(
        grads_kernel,
        out_shape=(
            jax.ShapeDtypeStruct((count // 2, width), F32),
            jax.ShapeDtypeStruct((count // 2, width), BF),
            jax.ShapeDtypeStruct((NG, NF * shard + hot_own, width), BF),
            jax.ShapeDtypeStruct((1, own), F32),
        ),
        in_specs=[smem] + [vmem] * (4 + len(rows)),
        scratch_shapes=[pltpu.VMEM((width, count), F32)],
        compiler_params=params,
    )(at_me, cold, mine, column, stats, *rows)

    near = lax.all_to_all(item_part, NEAR, 0, 0)
    keep = (keep + swap(send, "c").astype(F32)).reshape(4, own, width)
    sends = keep.astype(BF)
    others = [swap(sends[1], "z1"), swap(sends[2], "z2")]
    others.append(lax.ppermute(sends[3], ("z2", "z1"), [(i, 3 - i) for i in range(4)]))
    near, *others = lax.optimization_barrier((near, *others))
    near = jnp.sum(near.astype(F32), axis=0).astype(BF)
    cold_part = near[: NF * shard].reshape(NF, shard, width)
    hot_part = jnp.broadcast_to(near[None, NF * shard :], (NF, hot_own, width))
    far = lax.all_to_all(jnp.concatenate([cold_part, hot_part], axis=1), FAR, 0, 0)
    grad_queries = (keep[0] + sum(x.astype(F32) for x in others)).astype(BF)
    far, grad_queries = lax.optimization_barrier((far, grad_queries))
    grad_cold = jnp.sum(far[:, :shard].astype(F32), axis=0).astype(BF)
    grad_hot = jnp.sum(far[:, shard:].astype(F32), axis=0).astype(BF)
    grad_hot = spread(grad_hot, HALF).reshape(-1, width)
    grad_hot, grad_cold = lax.optimization_barrier((grad_hot, grad_cold))
    grad_hot = spread(grad_hot, NEAR)
    grad_hot = grad_hot.reshape(2, hot // 4, width)
    grad_hot = pl.pallas_call(
        place_kernel,
        out_shape=jax.ShapeDtypeStruct((hot, width), BF),
        in_specs=[vmem, vmem],
        out_specs=pl.BlockSpec(memory_space=pl.ANY),
        scratch_shapes=[pltpu.SemaphoreType.DMA((4,))],
        compiler_params=params,
    )(lax.all_gather(grad_hot[0], "c"), lax.all_gather(grad_hot[1], "c"))
    return grad_queries, grad_hot, grad_cold, loss[0]


def solution(mesh):
    fine = Mesh(mesh.devices.reshape((2,) * len(AXES)), AXES)
    rows = P(AXES, None)
    return jax.shard_map(
        body,
        mesh=fine,
        in_specs=(rows, P(), rows, P(), P()),
        out_specs=(rows, P(), rows, P(AXES)),
        check_vma=False,
    )
```

```python
import functools

import jax
import jax.numpy as jnp
from jax import lax
from jax.experimental import pallas as pl
from jax.experimental.pallas import tpu as pltpu
from jax.sharding import Mesh
from jax.sharding import PartitionSpec as P

AXES = ("z8", "z4", "z2", "z1", "yl", "c", "x2", "x1", "yh")
COLS = ("z2", "z1", "c")
HALF = ("z2", "z1")
NEAR = ("x2", "x1", "yh", "yl")
FAR = ("z8", "z4")
NC, NG, NF = 2 ** len(COLS), 2 ** len(NEAR), 2 ** len(FAR)
BF = jnp.bfloat16
F32 = jnp.float32
NT = (((1,), (1,)), ((), ()))
TN = (((0,), (0,)), ((), ()))
CHUNKS = 4


def spread(x, axes):
    n = lax.axis_size(axes)
    return lax.all_to_all(jnp.broadcast_to(x[None], (n, *x.shape)), axes, 0, 0)


def swap(x, axis):
    return lax.ppermute(x, axis, [(0, 1), (1, 0)])


def around(by_z1, by_z2, by_both):
    both = lax.ppermute(by_both, ("z2", "z1"), [(i, 3 - i) for i in range(4)])
    return swap(by_z1, "z1"), swap(by_z2, "z2"), both


def bit(index, axis):
    return (index >> (len(AXES) - 1 - AXES.index(axis))) & 1


def pick(index, axes):
    out = 0
    for a in axes:
        out = out * 2 + bit(index, a)
    return out


def flip(p):
    mask = 0
    for a in reversed(COLS):
        mask |= (p & 1) << (len(AXES) - 1 - AXES.index(a))
        p >>= 1
    return mask


def decode_kernel(me_ref, ids_ref, targets_ref, out_ref, aim_ref, sems):
    me = me_ref[0]
    k = pick(me, COLS)
    groups, lanes = ids_ref.shape
    copies = []
    for p in range(NC):
        here = aim_ref.at[:, pl.ds(p * lanes, lanes)]
        copies.append(pltpu.make_async_copy(targets_ref.at[me ^ flip(p)], here, sems.at[p]))
        copies[p].start()
    hot_own = groups * lanes // (NC * NG)
    shard = 32
    near_chunk = NG // CHUNKS
    width = near_chunk * (NF * shard + hot_own)
    for copy in copies:
        copy.wait()
    aim = aim_ref[...]
    below = jnp.zeros(aim.shape, jnp.int32)
    slot = jnp.zeros(aim.shape, jnp.int32)
    for i in range(groups):
        ids = jnp.broadcast_to(ids_ref[i : i + 1], (lanes, lanes)).T
        ids = jnp.concatenate([ids] * NC, axis=1)
        place = lax.broadcasted_iota(jnp.int32, ids.shape, 0) + (i * lanes + 1)
        below += jnp.sum((ids < aim).astype(jnp.int32), axis=0, keepdims=True)
        slot += jnp.sum(jnp.where(ids == aim, place, 0), axis=0, keepdims=True)
    slot -= 1
    is_hot = slot >= 0
    row = aim - below
    block = row >> 5
    near = pick(block, NEAR)
    cold_col = near // near_chunk * width + (near % near_chunk) * (NF * shard)
    cold_col += pick(block, FAR) * shard + (row & (shard - 1))
    hot_near = (slot >> 6) & (NG - 1)
    hot_k = (((slot >> 4) & 3) << 1) | (slot >> 10)
    hot_col = hot_near // near_chunk * width + near_chunk * NF * shard
    hot_col += (hot_near % near_chunk) * hot_own + (slot & (hot_own - 1))
    column = jnp.where(is_hot, hot_col, cold_col)
    there = jnp.where(is_hot, hot_k, pick(block, COLS))
    out_ref[...] = jnp.where(there == k, column, -1)


def chunk_table(cold_ref, hot_ref, g):
    n = NG // CHUNKS
    cold = cold_ref[pl.ds(g * n, n)]
    hot = hot_ref[pl.ds(g * n, n)]
    wide = cold.shape[-1]
    return jnp.concatenate([cold.reshape(-1, wide), hot.reshape(-1, wide)], axis=0)


def stats_kernel(me_ref, cold_ref, hot_ref, col_ref, *refs):
    *row_refs, out_ref = refs
    rows = jnp.concatenate([r[...] for r in row_refs], axis=0)
    cols = col_ref[...]
    count = rows.shape[0]
    k = pick(me_ref[0], COLS)

    def step(g, carry):
        top, total, hit = carry
        table = chunk_table(cold_ref, hot_ref, g)
        s = lax.dot_general(table, rows, NT, preferred_element_type=F32)
        new = jnp.maximum(top, jnp.max(s, axis=0, keepdims=True))
        total = total * jnp.exp(top - new) + jnp.sum(jnp.exp(s - new), axis=0, keepdims=True)
        where = lax.broadcasted_iota(jnp.int32, s.shape, 0) == cols - g * table.shape[0]
        hit = hit + jnp.sum(jnp.where(where, s, 0.0), axis=0, keepdims=True)
        return new, total, hit

    zero = jnp.zeros((1, count), F32)
    start = (jnp.full((1, count), -1e30, F32), zero, zero)
    top, total, hit = lax.fori_loop(0, CHUNKS, step, start, unroll=True)
    logs = top + jnp.log(total)
    for p in range(NC):
        here = slice(p * 128, (p + 1) * 128)
        there = pl.ds(pl.multiple_of((k ^ p) * 128, 128), 128)
        for d in range(NC):
            out_ref[d, 0:1, there] = logs[:, here]
            out_ref[d, 1:2, there] = hit[:, here]


def grads_kernel(me_ref, cold_ref, hot_ref, col_ref, stats_ref, *refs):
    *row_refs, keep_ref, send_1, send_2, send_3, item_ref, loss_ref, acc_ref = refs
    rows = jnp.concatenate([r[...] for r in row_refs], axis=0)
    cols = col_ref[...]
    k = pick(me_ref[0], COLS)
    pieces = []
    for p in range(NC):
        there = pl.ds(pl.multiple_of((k ^ p) * 128, 128), 128)
        tops = [stats_ref[d, 0:1, there] for d in range(NC)]
        top = functools.reduce(jnp.maximum, tops)
        total = sum(jnp.exp(t - top) for t in tops)
        pieces.append(top + jnp.log(total))
        if p == 0:
            loss_ref[...] = pieces[0] - sum(stats_ref[d, 1:2, there] for d in range(NC))
    logs = jnp.concatenate(pieces, axis=1)
    acc_ref[...] = jnp.zeros_like(acc_ref)
    n = NG // CHUNKS
    cold_rows = cold_ref.shape[1]

    def step(g, carry):
        table = chunk_table(cold_ref, hot_ref, g)
        s = lax.dot_general(table, rows, NT, preferred_element_type=F32)
        where = lax.broadcasted_iota(jnp.int32, s.shape, 0) == cols - g * table.shape[0]
        w = (jnp.exp(s - logs) - jnp.where(where, 1.0, 0.0)).astype(BF)
        item = jnp.dot(w, rows, preferred_element_type=F32).astype(BF)
        wide = item.shape[-1]
        item_ref[pl.ds(g * n, n), :cold_rows] = item[: n * cold_rows].reshape(n, -1, wide)
        item_ref[pl.ds(g * n, n), cold_rows:] = item[n * cold_rows :].reshape(n, -1, wide)
        acc_ref[...] += lax.dot_general(table, w, TN, preferred_element_type=F32)
        return carry

    lax.fori_loop(0, CHUNKS, step, 0, unroll=True)
    quarter = acc_ref.shape[1] // 4
    keep_ref[...] = acc_ref[:, :quarter].T
    for j, ref in enumerate((send_1, send_2, send_3)):
        ref[...] = acc_ref[:, (j + 1) * quarter : (j + 2) * quarter].T.astype(BF)


def place_kernel(me_ref, own_ref, other_ref, out_ref, sems):
    core = bit(me_ref[0], "c")
    half = own_ref.shape[0]
    first = pltpu.make_async_copy(own_ref, out_ref.at[pl.ds(core * half, half)], sems.at[0])
    second = pltpu.make_async_copy(
        other_ref, out_ref.at[pl.ds((1 - core) * half, half)], sems.at[1]
    )
    first.start()
    second.start()
    first.wait()
    second.wait()


def body(queries, hot_table, cold_table, hot_ids, targets):
    own, width = queries.shape
    shard = cold_table.shape[0]
    hot = hot_table.shape[0]
    hot_own = hot // (NC * NG)
    me = lax.axis_index(AXES)
    at_me = jnp.reshape(me, (1,)).astype(jnp.int32)
    k = pick(me, COLS)
    count = NC * own
    params = pltpu.CompilerParams(vmem_limit_bytes=24 << 20)
    vmem = pl.BlockSpec(memory_space=pltpu.VMEM)
    smem = pl.BlockSpec(memory_space=pltpu.SMEM)

    pair = jnp.concatenate([queries, swap(queries, "c")], axis=0)

    column = pl.pallas_call(
        decode_kernel,
        out_shape=jax.ShapeDtypeStruct((1, count), jnp.int32),
        in_specs=[smem, vmem, pl.BlockSpec(memory_space=pltpu.HBM)],
        scratch_shapes=[pltpu.VMEM((1, count), jnp.int32), pltpu.SemaphoreType.DMA((NC,))],
        cost_estimate=pl.CostEstimate(
            flops=6 * hot * count, bytes_accessed=1 << 20, transcendentals=0
        ),
        compiler_params=params,
    )(at_me, hot_ids.reshape(-1, 128), targets.reshape(-1, 1, own))

    far = spread(cold_table, FAR).reshape(NF * shard, width)
    far, pair = lax.optimization_barrier((far, pair))
    cold = spread(far, NEAR)
    rows = [pair, *around(pair, pair, pair)]
    rows[3], column = lax.optimization_barrier((rows[3], column))
    mine = hot_table.reshape(2, NG, NC // 2, hot_own, width)
    mine = lax.dynamic_slice(mine, (k & 1, 0, k >> 1, 0, 0), (1, NG, 1, hot_own, width))
    mine = mine.reshape(NG, hot_own, width)

    stats = pl.pallas_call(
        stats_kernel,
        out_shape=jax.ShapeDtypeStruct((NC, 2, count), F32),
        in_specs=[smem] + [vmem] * (3 + len(rows)),
        compiler_params=params,
    )(at_me, cold, mine, column, *rows)
    stats = lax.all_to_all(stats, COLS, 0, 0)
    keep, *sends, item_part, loss = pl.pallas_call(
        grads_kernel,
        out_shape=(
            jax.ShapeDtypeStruct((count // 4, width), F32),
            *[jax.ShapeDtypeStruct((count // 4, width), BF)] * 3,
            jax.ShapeDtypeStruct((NG, NF * shard + hot_own, width), BF),
            jax.ShapeDtypeStruct((1, own), F32),
        ),
        in_specs=[smem] + [vmem] * (4 + len(rows)),
        scratch_shapes=[pltpu.VMEM((width, count), F32)],
        compiler_params=params,
    )(at_me, cold, mine, column, stats, *rows)

    near = lax.all_to_all(item_part, NEAR, 0, 0)
    keep = keep + sum(x.astype(F32) for x in around(*sends))
    near, keep, other = lax.optimization_barrier((near, keep[:own], keep[own:].astype(BF)))
    near = jnp.sum(near.astype(F32), axis=0).astype(BF)
    cold_part = near[: NF * shard].reshape(NF, shard, width)
    hot_part = jnp.broadcast_to(near[None, NF * shard :], (NF, hot_own, width))
    far = lax.all_to_all(jnp.concatenate([cold_part, hot_part], axis=1), FAR, 0, 0)
    far = jnp.sum(far.astype(F32), axis=0).astype(BF)
    grad_cold = far[:shard]
    grad_hot = spread(far[shard:], HALF).reshape(-1, width)
    grad_hot = spread(grad_hot, NEAR)
    grad_hot, other = lax.optimization_barrier((grad_hot.reshape(hot // 2, width), other))
    grad_queries = (keep + swap(other, "c").astype(F32)).astype(BF)
    grad_hot = pl.pallas_call(
        place_kernel,
        out_shape=jax.ShapeDtypeStruct((hot, width), BF),
        in_specs=[smem, vmem, vmem],
        out_specs=pl.BlockSpec(memory_space=pl.ANY),
        scratch_shapes=[pltpu.SemaphoreType.DMA((2,))],
        compiler_params=params,
    )(at_me, grad_hot, swap(grad_hot, "c"))
    return grad_queries, grad_hot, grad_cold, loss[0]


def solution(mesh):
    fine = Mesh(mesh.devices.reshape((2,) * len(AXES)), AXES)
    rows = P(AXES, None)
    return jax.shard_map(
        body,
        mesh=fine,
        in_specs=(rows, P(), rows, P(), P()),
        out_specs=(rows, P(), rows, P(AXES)),
        check_vma=False,
    )
```

```python
import functools

import jax
import jax.numpy as jnp
from jax import lax
from jax.experimental import pallas as pl
from jax.experimental.pallas import tpu as pltpu
from jax.sharding import Mesh
from jax.sharding import PartitionSpec as P

AXES = ("z8", "z4", "z2", "z1", "yl", "c", "x2", "x1", "yh")
COLS = ("c", "z2", "z1")
HALF = ("z2", "z1")
NEAR = ("x2", "x1", "yh", "yl")
FAR = ("z8", "z4")
NC, NG, NF = 2 ** len(COLS), 2 ** len(NEAR), 2 ** len(FAR)
BF = jnp.bfloat16
F32 = jnp.float32
NT = (((1,), (1,)), ((), ()))
TN = (((0,), (0,)), ((), ()))
CHUNKS = 4


def spread(x, axes):
    n = lax.axis_size(axes)
    return lax.all_to_all(jnp.broadcast_to(x[None], (n, *x.shape)), axes, 0, 0)


def swap(x, axis):
    return lax.ppermute(x, axis, [(0, 1), (1, 0)])


def around(by_z1, by_z2, by_both):
    both = lax.ppermute(by_both, ("z2", "z1"), [(i, 3 - i) for i in range(4)])
    return swap(by_z1, "z1"), swap(by_z2, "z2"), both


def bit(index, axis):
    return (index >> (len(AXES) - 1 - AXES.index(axis))) & 1


def pick(index, axes):
    out = 0
    for a in axes:
        out = out * 2 + bit(index, a)
    return out


def flip(p):
    mask = 0
    for a in reversed(COLS):
        mask |= (p & 1) << (len(AXES) - 1 - AXES.index(a))
        p >>= 1
    return mask


def decode_kernel(me_ref, ids_ref, targets_ref, out_ref, aim_ref, sems):
    me = me_ref[0]
    k = pick(me, COLS)
    groups, lanes = ids_ref.shape
    copies = []
    for p in range(NC):
        here = aim_ref.at[:, pl.ds(p * lanes, lanes)]
        copies.append(pltpu.make_async_copy(targets_ref.at[me ^ flip(p)], here, sems.at[p]))
        copies[p].start()
    hot_own = groups * lanes // (NC * NG)
    shard = 32
    near_chunk = NG // CHUNKS
    width = near_chunk * (NF * shard + hot_own)
    for copy in copies:
        copy.wait()
    aim = aim_ref[...]
    below = jnp.zeros(aim.shape, jnp.int32)
    slot = jnp.zeros(aim.shape, jnp.int32)
    for i in range(groups):
        ids = jnp.broadcast_to(ids_ref[i : i + 1], (lanes, lanes)).T
        ids = jnp.concatenate([ids] * NC, axis=1)
        place = lax.broadcasted_iota(jnp.int32, ids.shape, 0) + (i * lanes + 1)
        below += jnp.sum((ids < aim).astype(jnp.int32), axis=0, keepdims=True)
        slot += jnp.sum(jnp.where(ids == aim, place, 0), axis=0, keepdims=True)
    slot -= 1
    is_hot = slot >= 0
    row = aim - below
    block = row >> 5
    near = pick(block, NEAR)
    cold_col = near // near_chunk * width + (near % near_chunk) * (NF * shard)
    cold_col += pick(block, FAR) * shard + (row & (shard - 1))
    hot_near = (slot >> 6) & (NG - 1)
    hot_k = ((slot >> 10) << 2) | ((slot >> 4) & 3)
    hot_col = hot_near // near_chunk * width + near_chunk * NF * shard
    hot_col += (hot_near % near_chunk) * hot_own + (slot & (hot_own - 1))
    column = jnp.where(is_hot, hot_col, cold_col)
    there = jnp.where(is_hot, hot_k, pick(block, COLS))
    out_ref[...] = jnp.where(there == k, column, -1)


def chunk_table(cold_ref, hot_ref, g):
    n = NG // CHUNKS
    cold = cold_ref[pl.ds(g * n, n)]
    hot = hot_ref[pl.ds(g * n, n)]
    wide = cold.shape[-1]
    return jnp.concatenate([cold.reshape(-1, wide), hot.reshape(-1, wide)], axis=0)


def stats_kernel(me_ref, cold_ref, hot_ref, col_ref, *refs):
    *row_refs, out_ref = refs
    rows = jnp.concatenate([r[...] for r in row_refs], axis=0)
    cols = col_ref[...]
    count = rows.shape[0]
    k = pick(me_ref[0], COLS)

    def step(g, carry):
        top, total, hit = carry
        table = chunk_table(cold_ref, hot_ref, g)
        s = lax.dot_general(table, rows, NT, preferred_element_type=F32)
        new = jnp.maximum(top, jnp.max(s, axis=0, keepdims=True))
        total = total * jnp.exp(top - new) + jnp.sum(jnp.exp(s - new), axis=0, keepdims=True)
        where = lax.broadcasted_iota(jnp.int32, s.shape, 0) == cols - g * table.shape[0]
        hit = hit + jnp.sum(jnp.where(where, s, 0.0), axis=0, keepdims=True)
        return new, total, hit

    zero = jnp.zeros((1, count), F32)
    start = (jnp.full((1, count), -1e30, F32), zero, zero)
    top, total, hit = lax.fori_loop(0, CHUNKS, step, start, unroll=True)
    logs = top + jnp.log(total)
    for p in range(NC):
        here = slice(p * 128, (p + 1) * 128)
        there = pl.ds(pl.multiple_of((k ^ p) * 128, 128), 128)
        for d in range(NC):
            out_ref[d, 0:1, there] = logs[:, here]
            out_ref[d, 1:2, there] = hit[:, here]


def grads_kernel(me_ref, cold_ref, hot_ref, col_ref, stats_ref, *refs):
    *row_refs, keep_ref, send_1, send_2, send_3, item_ref, loss_ref, acc_ref = refs
    rows = jnp.concatenate([r[...] for r in row_refs], axis=0)
    cols = col_ref[...]
    k = pick(me_ref[0], COLS)
    pieces = []
    for p in range(NC):
        there = pl.ds(pl.multiple_of((k ^ p) * 128, 128), 128)
        tops = [stats_ref[d, 0:1, there] for d in range(NC)]
        top = functools.reduce(jnp.maximum, tops)
        total = sum(jnp.exp(t - top) for t in tops)
        pieces.append(top + jnp.log(total))
        if p == 0:
            loss_ref[...] = pieces[0] - sum(stats_ref[d, 1:2, there] for d in range(NC))
    logs = jnp.concatenate(pieces, axis=1)
    acc_ref[...] = jnp.zeros_like(acc_ref)
    n = NG // CHUNKS
    cold_rows = cold_ref.shape[1]

    def step(g, carry):
        table = chunk_table(cold_ref, hot_ref, g)
        s = lax.dot_general(table, rows, NT, preferred_element_type=F32)
        where = lax.broadcasted_iota(jnp.int32, s.shape, 0) == cols - g * table.shape[0]
        w = (jnp.exp(s - logs) - jnp.where(where, 1.0, 0.0)).astype(BF)
        item = jnp.dot(w, rows, preferred_element_type=F32).astype(BF)
        wide = item.shape[-1]
        item_ref[pl.ds(g * n, n), :cold_rows] = item[: n * cold_rows].reshape(n, -1, wide)
        item_ref[pl.ds(g * n, n), cold_rows:] = item[n * cold_rows :].reshape(n, -1, wide)
        acc_ref[...] += lax.dot_general(table, w, TN, preferred_element_type=F32)
        return carry

    lax.fori_loop(0, CHUNKS, step, 0, unroll=True)
    own = acc_ref.shape[1] // NC
    for j, ref in enumerate((keep_ref, send_1, send_2, send_3)):
        for core in range(2):
            p = core * (NC // 2) + j
            part = acc_ref[:, p * own : (p + 1) * own].T
            ref[core * own : (core + 1) * own] = part.astype(ref.dtype)


def place_kernel(me_ref, own_ref, other_ref, out_ref, sems):
    core = bit(me_ref[0], "c")
    half = own_ref.shape[0]
    first = pltpu.make_async_copy(own_ref, out_ref.at[pl.ds(core * half, half)], sems.at[0])
    second = pltpu.make_async_copy(
        other_ref, out_ref.at[pl.ds((1 - core) * half, half)], sems.at[1]
    )
    first.start()
    second.start()
    first.wait()
    second.wait()


def body(queries, hot_table, cold_table, hot_ids, targets):
    own, width = queries.shape
    shard = cold_table.shape[0]
    hot = hot_table.shape[0]
    hot_own = hot // (NC * NG)
    me = lax.axis_index(AXES)
    at_me = jnp.reshape(me, (1,)).astype(jnp.int32)
    k = pick(me, COLS)
    count = NC * own
    params = pltpu.CompilerParams(vmem_limit_bytes=24 << 20)
    vmem = pl.BlockSpec(memory_space=pltpu.VMEM)
    smem = pl.BlockSpec(memory_space=pltpu.SMEM)

    rows = [queries, swap(queries, "z1")]

    column = pl.pallas_call(
        decode_kernel,
        out_shape=jax.ShapeDtypeStruct((1, count), jnp.int32),
        in_specs=[smem, vmem, pl.BlockSpec(memory_space=pltpu.HBM)],
        scratch_shapes=[pltpu.VMEM((1, count), jnp.int32), pltpu.SemaphoreType.DMA((NC,))],
        cost_estimate=pl.CostEstimate(
            flops=6 * hot * count, bytes_accessed=1 << 20, transcendentals=0
        ),
        compiler_params=params,
    )(at_me, hot_ids.reshape(-1, 128), targets.reshape(-1, 1, own))

    far = spread(cold_table, FAR).reshape(NF * shard, width)
    far, rows[1] = lax.optimization_barrier((far, rows[1]))
    cold = spread(far, NEAR)
    rows = jnp.concatenate(rows, axis=0)
    other, column = lax.optimization_barrier((swap(rows, "z2"), column))
    rows = jnp.concatenate([rows, other], axis=0)
    rows = [rows, swap(rows, "c")]
    mine = hot_table.reshape(2, NG, NC // 2, hot_own, width)
    mine = lax.dynamic_slice(mine, (k >> 2, 0, k & 3, 0, 0), (1, NG, 1, hot_own, width))
    mine = mine.reshape(NG, hot_own, width)

    stats = pl.pallas_call(
        stats_kernel,
        out_shape=jax.ShapeDtypeStruct((NC, 2, count), F32),
        in_specs=[smem] + [vmem] * (3 + len(rows)),
        compiler_params=params,
    )(at_me, cold, mine, column, *rows)
    stats = lax.all_to_all(stats, COLS, 0, 0)
    keep, *sends, item_part, loss = pl.pallas_call(
        grads_kernel,
        out_shape=(
            jax.ShapeDtypeStruct((count // 4, width), F32),
            *[jax.ShapeDtypeStruct((count // 4, width), BF)] * 3,
            jax.ShapeDtypeStruct((NG, NF * shard + hot_own, width), BF),
            jax.ShapeDtypeStruct((1, own), F32),
        ),
        in_specs=[smem] + [vmem] * (4 + len(rows)),
        scratch_shapes=[pltpu.VMEM((width, count), F32)],
        compiler_params=params,
    )(at_me, cold, mine, column, stats, *rows)

    near = lax.all_to_all(item_part, NEAR, 0, 0)
    keep = keep + sum(x.astype(F32) for x in around(*sends))
    near, keep, other = lax.optimization_barrier((near, keep[:own], keep[own:].astype(BF)))
    near = jnp.sum(near.astype(F32), axis=0).astype(BF)
    cold_part = near[: NF * shard].reshape(NF, shard, width)
    hot_part = jnp.broadcast_to(near[None, NF * shard :], (NF, hot_own, width))
    far = lax.all_to_all(jnp.concatenate([cold_part, hot_part], axis=1), FAR, 0, 0)
    far, other = lax.optimization_barrier((far, swap(other, "c")))
    grad_queries = (keep + other.astype(F32)).astype(BF)
    far = jnp.sum(far.astype(F32), axis=0).astype(BF)
    grad_cold = far[:shard]
    grad_hot = spread(far[shard:], HALF).reshape(-1, width)
    grad_hot = spread(grad_hot, NEAR)
    grad_hot = grad_hot.reshape(hot // 2, width)
    grad_hot = pl.pallas_call(
        place_kernel,
        out_shape=jax.ShapeDtypeStruct((hot, width), BF),
        in_specs=[smem, vmem, vmem],
        out_specs=pl.BlockSpec(memory_space=pl.ANY),
        scratch_shapes=[pltpu.SemaphoreType.DMA((2,))],
        compiler_params=params,
    )(at_me, grad_hot, swap(grad_hot, "c"))
    return grad_queries, grad_hot, grad_cold, loss[0]


def solution(mesh):
    fine = Mesh(mesh.devices.reshape((2,) * len(AXES)), AXES)
    rows = P(AXES, None)
    return jax.shard_map(
        body,
        mesh=fine,
        in_specs=(rows, P(), rows, P(), P()),
        out_specs=(rows, P(), rows, P(AXES)),
        check_vma=False,
    )
```

```python
import functools

import jax
import jax.numpy as jnp
from jax import lax
from jax.experimental import pallas as pl
from jax.experimental.pallas import tpu as pltpu
from jax.sharding import Mesh
from jax.sharding import PartitionSpec as P

AXES = ("z8", "z4", "z2", "z1", "yl", "c", "x2", "x1", "yh")
COLS = ("c", "z2", "z1")
HALF = ("z2", "z1")
NEAR = ("x2", "x1", "yh", "yl")
FAR = ("z8", "z4")
NC, NG, NF = 2 ** len(COLS), 2 ** len(NEAR), 2 ** len(FAR)
BF = jnp.bfloat16
F32 = jnp.float32
NT = (((1,), (1,)), ((), ()))
TN = (((0,), (0,)), ((), ()))
CHUNKS = 4


def spread(x, axes):
    n = lax.axis_size(axes)
    return lax.all_to_all(jnp.broadcast_to(x[None], (n, *x.shape)), axes, 0, 0)


def swap(x, axis):
    return lax.ppermute(x, axis, [(0, 1), (1, 0)])


def around(by_z1, by_z2, by_both):
    both = lax.ppermute(by_both, ("z2", "z1"), [(i, 3 - i) for i in range(4)])
    return swap(by_z1, "z1"), swap(by_z2, "z2"), both


def bit(index, axis):
    return (index >> (len(AXES) - 1 - AXES.index(axis))) & 1


def pick(index, axes):
    out = 0
    for a in axes:
        out = out * 2 + bit(index, a)
    return out


def flip(p):
    mask = 0
    for a in reversed(COLS):
        mask |= (p & 1) << (len(AXES) - 1 - AXES.index(a))
        p >>= 1
    return mask


def decode_kernel(me_ref, ids_ref, targets_ref, out_ref, aim_ref, sems):
    me = me_ref[0]
    k = pick(me, COLS)
    groups, lanes = ids_ref.shape
    copies = []
    for p in range(NC):
        here = aim_ref.at[:, pl.ds(p * lanes, lanes)]
        copies.append(pltpu.make_async_copy(targets_ref.at[me ^ flip(p)], here, sems.at[p]))
        copies[p].start()
    hot_own = groups * lanes // (NC * NG)
    shard = 32
    near_chunk = NG // CHUNKS
    width = near_chunk * (NF * shard + hot_own)
    for copy in copies:
        copy.wait()
    aim = aim_ref[...]
    below = jnp.zeros(aim.shape, jnp.int32)
    slot = jnp.zeros(aim.shape, jnp.int32)
    for i in range(groups):
        ids = jnp.broadcast_to(ids_ref[i : i + 1], (lanes, lanes)).T
        ids = jnp.concatenate([ids] * NC, axis=1)
        place = lax.broadcasted_iota(jnp.int32, ids.shape, 0) + (i * lanes + 1)
        below += jnp.sum((ids < aim).astype(jnp.int32), axis=0, keepdims=True)
        slot += jnp.sum(jnp.where(ids == aim, place, 0), axis=0, keepdims=True)
    slot -= 1
    is_hot = slot >= 0
    row = aim - below
    block = row >> 5
    near = pick(block, NEAR)
    cold_col = near // near_chunk * width + (near % near_chunk) * (NF * shard)
    cold_col += pick(block, FAR) * shard + (row & (shard - 1))
    hot_near = (slot >> 6) & (NG - 1)
    hot_k = ((slot >> 10) << 2) | ((slot >> 4) & 3)
    hot_col = hot_near // near_chunk * width + near_chunk * NF * shard
    hot_col += (hot_near % near_chunk) * hot_own + (slot & (hot_own - 1))
    column = jnp.where(is_hot, hot_col, cold_col)
    there = jnp.where(is_hot, hot_k, pick(block, COLS))
    out_ref[...] = jnp.where(there == k, column, -1)


def chunk_table(cold_ref, hot_ref, g):
    n = NG // CHUNKS
    cold = cold_ref[pl.ds(g * n, n)]
    hot = hot_ref[pl.ds(g * n, n)]
    wide = cold.shape[-1]
    return jnp.concatenate([cold.reshape(-1, wide), hot.reshape(-1, wide)], axis=0)


def stats_kernel(me_ref, cold_ref, hot_ref, col_ref, *refs):
    *row_refs, out_ref = refs
    rows = jnp.concatenate([r[...] for r in row_refs], axis=0)
    cols = col_ref[...]
    count = rows.shape[0]
    k = pick(me_ref[0], COLS)

    def step(g, carry):
        top, total, hit = carry
        table = chunk_table(cold_ref, hot_ref, g)
        s = lax.dot_general(table, rows, NT, preferred_element_type=F32)
        new = jnp.maximum(top, jnp.max(s, axis=0, keepdims=True))
        total = total * jnp.exp(top - new) + jnp.sum(jnp.exp(s - new), axis=0, keepdims=True)
        where = lax.broadcasted_iota(jnp.int32, s.shape, 0) == cols - g * table.shape[0]
        hit = hit + jnp.sum(jnp.where(where, s, 0.0), axis=0, keepdims=True)
        return new, total, hit

    zero = jnp.zeros((1, count), F32)
    start = (jnp.full((1, count), -1e30, F32), zero, zero)
    top, total, hit = lax.fori_loop(0, CHUNKS, step, start, unroll=True)
    logs = top + jnp.log(total)
    for p in range(NC):
        here = slice(p * 128, (p + 1) * 128)
        there = pl.ds(pl.multiple_of((k ^ p) * 128, 128), 128)
        for d in range(NC):
            out_ref[d, 0:1, there] = logs[:, here]
            out_ref[d, 1:2, there] = hit[:, here]


def grads_kernel(me_ref, cold_ref, hot_ref, col_ref, stats_ref, *refs):
    *row_refs, keep_ref, send_1, send_2, send_3, item_ref, loss_ref, acc_ref = refs
    rows = jnp.concatenate([r[...] for r in row_refs], axis=0)
    cols = col_ref[...]
    k = pick(me_ref[0], COLS)
    pieces = []
    for p in range(NC):
        there = pl.ds(pl.multiple_of((k ^ p) * 128, 128), 128)
        tops = [stats_ref[d, 0:1, there] for d in range(NC)]
        top = functools.reduce(jnp.maximum, tops)
        total = sum(jnp.exp(t - top) for t in tops)
        pieces.append(top + jnp.log(total))
        if p == 0:
            loss_ref[...] = pieces[0] - sum(stats_ref[d, 1:2, there] for d in range(NC))
    logs = jnp.concatenate(pieces, axis=1)
    acc_ref[...] = jnp.zeros_like(acc_ref)
    n = NG // CHUNKS
    cold_rows = cold_ref.shape[1]

    def step(g, carry):
        table = chunk_table(cold_ref, hot_ref, g)
        s = lax.dot_general(table, rows, NT, preferred_element_type=F32)
        where = lax.broadcasted_iota(jnp.int32, s.shape, 0) == cols - g * table.shape[0]
        w = (jnp.exp(s - logs) - jnp.where(where, 1.0, 0.0)).astype(BF)
        item = jnp.dot(w, rows, preferred_element_type=F32).astype(BF)
        wide = item.shape[-1]
        item_ref[pl.ds(g * n, n), :cold_rows] = item[: n * cold_rows].reshape(n, -1, wide)
        item_ref[pl.ds(g * n, n), cold_rows:] = item[n * cold_rows :].reshape(n, -1, wide)
        acc_ref[...] += lax.dot_general(table, w, TN, preferred_element_type=F32)
        return carry

    lax.fori_loop(0, CHUNKS, step, 0, unroll=True)
    own = acc_ref.shape[1] // NC
    for j, ref in enumerate((keep_ref, send_1, send_2, send_3)):
        for core in range(2):
            p = core * (NC // 2) + j
            part = acc_ref[:, p * own : (p + 1) * own].T
            ref[core * own : (core + 1) * own] = part.astype(ref.dtype)


def place_kernel(me_ref, own_ref, other_ref, keep_ref, out_ref, query_ref, sems):
    core = bit(me_ref[0], "c")
    half = own_ref.shape[0]
    first = pltpu.make_async_copy(own_ref, out_ref.at[pl.ds(core * half, half)], sems.at[0])
    second = pltpu.make_async_copy(
        other_ref.at[pl.ds(0, half)], out_ref.at[pl.ds((1 - core) * half, half)], sems.at[1]
    )
    first.start()
    second.start()
    query_ref[...] = (keep_ref[...] + other_ref[half:].astype(F32)).astype(query_ref.dtype)
    first.wait()
    second.wait()


def body(queries, hot_table, cold_table, hot_ids, targets):
    own, width = queries.shape
    shard = cold_table.shape[0]
    hot = hot_table.shape[0]
    hot_own = hot // (NC * NG)
    me = lax.axis_index(AXES)
    at_me = jnp.reshape(me, (1,)).astype(jnp.int32)
    k = pick(me, COLS)
    count = NC * own
    params = pltpu.CompilerParams(vmem_limit_bytes=24 << 20)
    vmem = pl.BlockSpec(memory_space=pltpu.VMEM)
    smem = pl.BlockSpec(memory_space=pltpu.SMEM)

    rows = [queries, swap(queries, "z1")]

    column = pl.pallas_call(
        decode_kernel,
        out_shape=jax.ShapeDtypeStruct((1, count), jnp.int32),
        in_specs=[smem, vmem, pl.BlockSpec(memory_space=pltpu.HBM)],
        scratch_shapes=[pltpu.VMEM((1, count), jnp.int32), pltpu.SemaphoreType.DMA((NC,))],
        cost_estimate=pl.CostEstimate(
            flops=6 * hot * count, bytes_accessed=1 << 20, transcendentals=0
        ),
        compiler_params=params,
    )(at_me, hot_ids.reshape(-1, 128), targets.reshape(-1, 1, own))

    far = spread(cold_table, FAR).reshape(NF * shard, width)
    far, rows[1] = lax.optimization_barrier((far, rows[1]))
    cold = spread(far, NEAR)
    rows = jnp.concatenate(rows, axis=0)
    other, column = lax.optimization_barrier((swap(rows, "z2"), column))
    rows = jnp.concatenate([rows, other], axis=0)
    rows = [rows, swap(rows, "c")]
    mine = hot_table.reshape(2, NG, NC // 2, hot_own, width)
    mine = lax.dynamic_slice(mine, (k >> 2, 0, k & 3, 0, 0), (1, NG, 1, hot_own, width))
    mine = mine.reshape(NG, hot_own, width)

    stats = pl.pallas_call(
        stats_kernel,
        out_shape=jax.ShapeDtypeStruct((NC, 2, count), F32),
        in_specs=[smem] + [vmem] * (3 + len(rows)),
        compiler_params=params,
    )(at_me, cold, mine, column, *rows)
    stats = lax.all_to_all(stats, COLS, 0, 0)
    keep, *sends, item_part, loss = pl.pallas_call(
        grads_kernel,
        out_shape=(
            jax.ShapeDtypeStruct((count // 4, width), F32),
            *[jax.ShapeDtypeStruct((count // 4, width), BF)] * 3,
            jax.ShapeDtypeStruct((NG, NF * shard + hot_own, width), BF),
            jax.ShapeDtypeStruct((1, own), F32),
        ),
        in_specs=[smem] + [vmem] * (4 + len(rows)),
        scratch_shapes=[pltpu.VMEM((width, count), F32)],
        compiler_params=params,
    )(at_me, cold, mine, column, stats, *rows)

    near = lax.all_to_all(item_part, NEAR, 0, 0)
    keep = keep + sum(x.astype(F32) for x in around(*sends))
    near, keep, other = lax.optimization_barrier((near, keep[:own], keep[own:].astype(BF)))
    near = jnp.sum(near.astype(F32), axis=0).astype(BF)
    cold_part = near[: NF * shard].reshape(NF, shard, width)
    hot_part = jnp.broadcast_to(near[None, NF * shard :], (NF, hot_own, width))
    far = lax.all_to_all(jnp.concatenate([cold_part, hot_part], axis=1), FAR, 0, 0)
    far = jnp.sum(far.astype(F32), axis=0).astype(BF)
    grad_cold = far[:shard]
    grad_hot = spread(far[shard:], HALF).reshape(-1, width)
    grad_hot = spread(grad_hot, NEAR)
    grad_hot = grad_hot.reshape(hot // 2, width)
    swapped = swap(jnp.concatenate([grad_hot, other], axis=0), "c")
    grad_hot, grad_queries = pl.pallas_call(
        place_kernel,
        out_shape=(
            jax.ShapeDtypeStruct((hot, width), BF),
            jax.ShapeDtypeStruct((own, width), BF),
        ),
        in_specs=[smem, vmem, vmem, vmem],
        out_specs=(pl.BlockSpec(memory_space=pl.ANY), vmem),
        scratch_shapes=[pltpu.SemaphoreType.DMA((2,))],
        compiler_params=params,
    )(at_me, grad_hot, swapped, keep)
    return grad_queries, grad_hot, grad_cold, loss[0]


def solution(mesh):
    fine = Mesh(mesh.devices.reshape((2,) * len(AXES)), AXES)
    rows = P(AXES, None)
    return jax.shard_map(
        body,
        mesh=fine,
        in_specs=(rows, P(), rows, P(), P()),
        out_specs=(rows, P(), rows, P(AXES)),
        check_vma=False,
    )
```

```python
import functools

import jax
import jax.numpy as jnp
from jax import lax
from jax.experimental import pallas as pl
from jax.experimental.pallas import tpu as pltpu
from jax.sharding import Mesh
from jax.sharding import PartitionSpec as P

AXES = ("z8", "z4", "z2", "z1", "yl", "c", "x2", "x1", "yh")
COLS = ("c", "z2", "z1")
HALF = ("z2", "z1")
NEAR = ("x2", "x1", "yh", "yl")
FAR = ("z8", "z4")
NC, NG, NF = 2 ** len(COLS), 2 ** len(NEAR), 2 ** len(FAR)
BF = jnp.bfloat16
F32 = jnp.float32
NT = (((1,), (1,)), ((), ()))
TN = (((0,), (0,)), ((), ()))
CHUNKS = 4


def spread(x, axes):
    n = lax.axis_size(axes)
    return lax.all_to_all(jnp.broadcast_to(x[None], (n, *x.shape)), axes, 0, 0)


def swap(x, axis):
    return lax.ppermute(x, axis, [(0, 1), (1, 0)])


def around(by_z1, by_z2, by_both):
    both = lax.ppermute(by_both, ("z2", "z1"), [(i, 3 - i) for i in range(4)])
    return swap(by_z1, "z1"), swap(by_z2, "z2"), both


def bit(index, axis):
    return (index >> (len(AXES) - 1 - AXES.index(axis))) & 1


def pick(index, axes):
    out = 0
    for a in axes:
        out = out * 2 + bit(index, a)
    return out


def flip(p):
    mask = 0
    for a in reversed(COLS):
        mask |= (p & 1) << (len(AXES) - 1 - AXES.index(a))
        p >>= 1
    return mask


def decode_kernel(me_ref, ids_ref, targets_ref, out_ref, aim_ref, sems):
    me = me_ref[0]
    k = pick(me, COLS)
    groups, lanes = ids_ref.shape
    copies = []
    for p in range(NC):
        here = aim_ref.at[:, pl.ds(p * lanes, lanes)]
        copies.append(pltpu.make_async_copy(targets_ref.at[me ^ flip(p)], here, sems.at[p]))
        copies[p].start()
    hot_own = groups * lanes // (NC * NG)
    shard = 32
    near_chunk = NG // CHUNKS
    width = near_chunk * (NF * shard + hot_own)
    for copy in copies:
        copy.wait()
    aim = aim_ref[...]
    below = jnp.zeros(aim.shape, jnp.int32)
    slot = jnp.zeros(aim.shape, jnp.int32)
    for i in range(groups):
        ids = jnp.broadcast_to(ids_ref[i : i + 1], (lanes, lanes)).T
        ids = jnp.concatenate([ids] * NC, axis=1)
        place = lax.broadcasted_iota(jnp.int32, ids.shape, 0) + (i * lanes + 1)
        below += jnp.sum((ids < aim).astype(jnp.int32), axis=0, keepdims=True)
        slot += jnp.sum(jnp.where(ids == aim, place, 0), axis=0, keepdims=True)
    slot -= 1
    is_hot = slot >= 0
    row = aim - below
    block = row >> 5
    near = pick(block, NEAR)
    cold_col = near // near_chunk * width + (near % near_chunk) * (NF * shard)
    cold_col += pick(block, FAR) * shard + (row & (shard - 1))
    hot_near = (slot >> 6) & (NG - 1)
    hot_k = ((slot >> 10) << 2) | ((slot >> 4) & 3)
    hot_col = hot_near // near_chunk * width + near_chunk * NF * shard
    hot_col += (hot_near % near_chunk) * hot_own + (slot & (hot_own - 1))
    column = jnp.where(is_hot, hot_col, cold_col)
    there = jnp.where(is_hot, hot_k, pick(block, COLS))
    out_ref[...] = jnp.where(there == k, column, -1)


def chunk_table(cold_ref, hot_ref, g):
    n = NG // CHUNKS
    cold = cold_ref[pl.ds(g * n, n)]
    hot = hot_ref[pl.ds(g * n, n)]
    wide = cold.shape[-1]
    return jnp.concatenate([cold.reshape(-1, wide), hot.reshape(-1, wide)], axis=0)


def stats_kernel(me_ref, cold_ref, hot_ref, col_ref, *refs):
    *row_refs, out_ref = refs
    rows = jnp.concatenate([r[...] for r in row_refs], axis=0)
    cols = col_ref[...]
    count = rows.shape[0]
    k = pick(me_ref[0], COLS)

    def step(g, carry):
        top, total, hit = carry
        table = chunk_table(cold_ref, hot_ref, g)
        s = lax.dot_general(table, rows, NT, preferred_element_type=F32)
        new = jnp.maximum(top, jnp.max(s, axis=0, keepdims=True))
        total = total * jnp.exp(top - new) + jnp.sum(jnp.exp(s - new), axis=0, keepdims=True)
        where = lax.broadcasted_iota(jnp.int32, s.shape, 0) == cols - g * table.shape[0]
        hit = hit + jnp.sum(jnp.where(where, s, 0.0), axis=0, keepdims=True)
        return new, total, hit

    zero = jnp.zeros((1, count), F32)
    start = (jnp.full((1, count), -1e30, F32), zero, zero)
    top, total, hit = lax.fori_loop(0, CHUNKS, step, start, unroll=True)
    logs = top + jnp.log(total)
    for p in range(NC):
        here = slice(p * 128, (p + 1) * 128)
        there = pl.ds(pl.multiple_of((k ^ p) * 128, 128), 128)
        for d in range(NC):
            out_ref[d, 0:1, there] = logs[:, here]
            out_ref[d, 1:2, there] = hit[:, here]


def grads_kernel(me_ref, cold_ref, hot_ref, col_ref, stats_ref, *refs):
    *row_refs, keep_ref, send_1, send_2, send_3, out_ref, loss_ref, acc_ref, item_ref, sems = refs
    rows = jnp.concatenate([r[...] for r in row_refs], axis=0)
    cols = col_ref[...]
    k = pick(me_ref[0], COLS)
    pieces = []
    for p in range(NC):
        there = pl.ds(pl.multiple_of((k ^ p) * 128, 128), 128)
        tops = [stats_ref[d, 0:1, there] for d in range(NC)]
        top = functools.reduce(jnp.maximum, tops)
        total = sum(jnp.exp(t - top) for t in tops)
        pieces.append(top + jnp.log(total))
        if p == 0:
            loss_ref[...] = pieces[0] - sum(stats_ref[d, 1:2, there] for d in range(NC))
    logs = jnp.concatenate(pieces, axis=1)
    acc_ref[...] = jnp.zeros_like(acc_ref)
    n = NG // CHUNKS
    cold_rows = cold_ref.shape[1]

    def copy_out(g):
        there = pl.ds(g * n, n)
        return pltpu.make_async_copy(item_ref.at[there], out_ref.at[there], sems.at[g])

    def step(g, carry):
        table = chunk_table(cold_ref, hot_ref, g)
        s = lax.dot_general(table, rows, NT, preferred_element_type=F32)
        where = lax.broadcasted_iota(jnp.int32, s.shape, 0) == cols - g * table.shape[0]
        w = (jnp.exp(s - logs) - jnp.where(where, 1.0, 0.0)).astype(BF)
        item = jnp.dot(w, rows, preferred_element_type=F32).astype(BF)
        wide = item.shape[-1]
        item_ref[pl.ds(g * n, n), :cold_rows] = item[: n * cold_rows].reshape(n, -1, wide)
        item_ref[pl.ds(g * n, n), cold_rows:] = item[n * cold_rows :].reshape(n, -1, wide)
        copy_out(g).start()
        acc_ref[...] += lax.dot_general(table, w, TN, preferred_element_type=F32)
        return carry

    lax.fori_loop(0, CHUNKS, step, 0, unroll=True)
    own = acc_ref.shape[1] // NC
    for j, ref in enumerate((keep_ref, send_1, send_2, send_3)):
        for core in range(2):
            p = core * (NC // 2) + j
            part = acc_ref[:, p * own : (p + 1) * own].T
            ref[core * own : (core + 1) * own] = part.astype(ref.dtype)
    for g in range(CHUNKS):
        copy_out(g).wait()


def place_kernel(me_ref, own_ref, other_ref, keep_ref, out_ref, query_ref, sum_ref, sems):
    core = bit(me_ref[0], "c")
    half = own_ref.shape[0]
    first = pltpu.make_async_copy(own_ref, out_ref.at[pl.ds(core * half, half)], sems.at[0])
    second = pltpu.make_async_copy(
        other_ref.at[pl.ds(0, half)], out_ref.at[pl.ds((1 - core) * half, half)], sems.at[1]
    )
    first.start()
    second.start()
    sum_ref[...] = (keep_ref[...] + other_ref[half:].astype(F32)).astype(sum_ref.dtype)
    third = pltpu.make_async_copy(sum_ref, query_ref, sems.at[2])
    third.start()
    first.wait()
    second.wait()
    third.wait()


def body(queries, hot_table, cold_table, hot_ids, targets):
    own, width = queries.shape
    shard = cold_table.shape[0]
    hot = hot_table.shape[0]
    hot_own = hot // (NC * NG)
    me = lax.axis_index(AXES)
    at_me = jnp.reshape(me, (1,)).astype(jnp.int32)
    k = pick(me, COLS)
    count = NC * own
    params = pltpu.CompilerParams(vmem_limit_bytes=24 << 20)
    vmem = pl.BlockSpec(memory_space=pltpu.VMEM)
    smem = pl.BlockSpec(memory_space=pltpu.SMEM)

    rows = [queries, swap(queries, "z1")]

    column = pl.pallas_call(
        decode_kernel,
        out_shape=jax.ShapeDtypeStruct((1, count), jnp.int32),
        in_specs=[smem, vmem, pl.BlockSpec(memory_space=pltpu.HBM)],
        scratch_shapes=[pltpu.VMEM((1, count), jnp.int32), pltpu.SemaphoreType.DMA((NC,))],
        cost_estimate=pl.CostEstimate(
            flops=6 * hot * count, bytes_accessed=1 << 20, transcendentals=0
        ),
        compiler_params=params,
    )(at_me, hot_ids.reshape(-1, 128), targets.reshape(-1, 1, own))

    far = spread(cold_table, FAR).reshape(NF * shard, width)
    far, rows[1] = lax.optimization_barrier((far, rows[1]))
    cold = spread(far, NEAR)
    rows = jnp.concatenate(rows, axis=0)
    other, column = lax.optimization_barrier((swap(rows, "z2"), column))
    rows = jnp.concatenate([rows, other], axis=0)
    rows = [rows, swap(rows, "c")]
    mine = hot_table.reshape(2, NG, NC // 2, hot_own, width)
    mine = lax.dynamic_slice(mine, (k >> 2, 0, k & 3, 0, 0), (1, NG, 1, hot_own, width))
    mine = mine.reshape(NG, hot_own, width)

    stats = pl.pallas_call(
        stats_kernel,
        out_shape=jax.ShapeDtypeStruct((NC, 2, count), F32),
        in_specs=[smem] + [vmem] * (3 + len(rows)),
        compiler_params=params,
    )(at_me, cold, mine, column, *rows)
    stats = lax.all_to_all(stats, COLS, 0, 0)
    keep, *sends, item_part, loss = pl.pallas_call(
        grads_kernel,
        out_shape=(
            jax.ShapeDtypeStruct((count // 4, width), F32),
            *[jax.ShapeDtypeStruct((count // 4, width), BF)] * 3,
            jax.ShapeDtypeStruct((NG, NF * shard + hot_own, width), BF),
            jax.ShapeDtypeStruct((1, own), F32),
        ),
        in_specs=[smem] + [vmem] * (4 + len(rows)),
        out_specs=(vmem, vmem, vmem, vmem, pl.BlockSpec(memory_space=pl.ANY), vmem),
        scratch_shapes=[
            pltpu.VMEM((width, count), F32),
            pltpu.VMEM((NG, NF * shard + hot_own, width), BF),
            pltpu.SemaphoreType.DMA((CHUNKS,)),
        ],
        compiler_params=params,
    )(at_me, cold, mine, column, stats, *rows)

    near = lax.all_to_all(item_part, NEAR, 0, 0)
    keep = keep + sum(x.astype(F32) for x in around(*sends))
    near, keep, other = lax.optimization_barrier((near, keep[:own], keep[own:].astype(BF)))
    near = jnp.sum(near.astype(F32), axis=0).astype(BF)
    cold_part = near[: NF * shard].reshape(NF, shard, width)
    hot_part = jnp.broadcast_to(near[None, NF * shard :], (NF, hot_own, width))
    far = lax.all_to_all(jnp.concatenate([cold_part, hot_part], axis=1), FAR, 0, 0)
    far = jnp.sum(far.astype(F32), axis=0).astype(BF)
    grad_cold = far[:shard]
    grad_hot = spread(far[shard:], HALF).reshape(-1, width)
    grad_hot = spread(grad_hot, NEAR)
    grad_hot = grad_hot.reshape(hot // 2, width)
    swapped = swap(jnp.concatenate([grad_hot, other], axis=0), "c")
    grad_hot, grad_queries = pl.pallas_call(
        place_kernel,
        out_shape=(
            jax.ShapeDtypeStruct((hot, width), BF),
            jax.ShapeDtypeStruct((own, width), BF),
        ),
        in_specs=[smem, vmem, vmem, vmem],
        out_specs=(pl.BlockSpec(memory_space=pl.ANY),) * 2,
        scratch_shapes=[pltpu.VMEM((own, width), BF), pltpu.SemaphoreType.DMA((3,))],
        compiler_params=params,
    )(at_me, grad_hot, swapped, keep)
    return grad_queries, grad_hot, grad_cold, loss[0]


def solution(mesh):
    fine = Mesh(mesh.devices.reshape((2,) * len(AXES)), AXES)
    rows = P(AXES, None)
    return jax.shard_map(
        body,
        mesh=fine,
        in_specs=(rows, P(), rows, P(), P()),
        out_specs=(rows, P(), rows, P(AXES)),
        check_vma=False,
    )
```

```python
import functools

import jax
import jax.numpy as jnp
from jax import lax
from jax.experimental import pallas as pl
from jax.experimental.pallas import tpu as pltpu
from jax.sharding import Mesh
from jax.sharding import PartitionSpec as P

AXES = ("z8", "z4", "z2", "z1", "yl", "c", "x2", "x1", "yh")
COLS = ("c", "z2", "z1")
HALF = ("z2", "z1")
NEAR = ("x2", "x1", "yh", "yl")
FAR = ("z8", "z4")
NC, NG, NF = 2 ** len(COLS), 2 ** len(NEAR), 2 ** len(FAR)
BF = jnp.bfloat16
F32 = jnp.float32
NT = (((1,), (1,)), ((), ()))
TN = (((0,), (0,)), ((), ()))
CHUNKS = 4


def spread(x, axes):
    n = lax.axis_size(axes)
    return lax.all_to_all(jnp.broadcast_to(x[None], (n, *x.shape)), axes, 0, 0)


def swap(x, axis):
    return lax.ppermute(x, axis, [(0, 1), (1, 0)])


def around(by_z1, by_z2, by_both):
    both = lax.ppermute(by_both, ("z2", "z1"), [(i, 3 - i) for i in range(4)])
    return swap(by_z1, "z1"), swap(by_z2, "z2"), both


def bit(index, axis):
    return (index >> (len(AXES) - 1 - AXES.index(axis))) & 1


def pick(index, axes):
    out = 0
    for a in axes:
        out = out * 2 + bit(index, a)
    return out


def flip(p):
    mask = 0
    for a in reversed(COLS):
        mask |= (p & 1) << (len(AXES) - 1 - AXES.index(a))
        p >>= 1
    return mask


def decode_kernel(me_ref, ids_ref, targets_ref, out_ref, aim_ref, sems):
    me = me_ref[0]
    k = pick(me, COLS)
    groups, lanes = ids_ref.shape
    copies = []
    for p in range(NC):
        here = aim_ref.at[:, pl.ds(p * lanes, lanes)]
        copies.append(pltpu.make_async_copy(targets_ref.at[me ^ flip(p)], here, sems.at[p]))
        copies[p].start()
    hot_own = groups * lanes // (NC * NG)
    shard = 32
    near_chunk = NG // CHUNKS
    width = near_chunk * (NF * shard + hot_own)
    for copy in copies:
        copy.wait()
    aim = aim_ref[...]
    below = jnp.zeros(aim.shape, jnp.int32)
    slot = jnp.zeros(aim.shape, jnp.int32)
    for i in range(groups):
        ids = jnp.broadcast_to(ids_ref[i : i + 1], (lanes, lanes)).T
        ids = jnp.concatenate([ids] * NC, axis=1)
        place = lax.broadcasted_iota(jnp.int32, ids.shape, 0) + (i * lanes + 1)
        below += jnp.sum((ids < aim).astype(jnp.int32), axis=0, keepdims=True)
        slot += jnp.sum(jnp.where(ids == aim, place, 0), axis=0, keepdims=True)
    slot -= 1
    is_hot = slot >= 0
    row = aim - below
    block = row >> 5
    near = pick(block, NEAR)
    cold_col = near // near_chunk * width + (near % near_chunk) * (NF * shard)
    cold_col += pick(block, FAR) * shard + (row & (shard - 1))
    hot_near = (slot >> 6) & (NG - 1)
    hot_k = ((slot >> 10) << 2) | ((slot >> 4) & 3)
    hot_col = hot_near // near_chunk * width + near_chunk * NF * shard
    hot_col += (hot_near % near_chunk) * hot_own + (slot & (hot_own - 1))
    column = jnp.where(is_hot, hot_col, cold_col)
    there = jnp.where(is_hot, hot_k, pick(block, COLS))
    out_ref[...] = jnp.where(there == k, column, -1)


def chunk_table(cold_ref, hot_ref, g):
    n = NG // CHUNKS
    cold = cold_ref[pl.ds(g * n, n)]
    hot = hot_ref[pl.ds(g * n, n)]
    wide = cold.shape[-1]
    return jnp.concatenate([cold.reshape(-1, wide), hot.reshape(-1, wide)], axis=0)


def stats_kernel(me_ref, cold_ref, hot_ref, col_ref, *refs):
    *row_refs, out_ref = refs
    rows = jnp.concatenate([r[...] for r in row_refs], axis=0)
    cols = col_ref[...]
    count = rows.shape[0]
    k = pick(me_ref[0], COLS)

    def step(g, carry):
        top, total, hit = carry
        table = chunk_table(cold_ref, hot_ref, g)
        s = lax.dot_general(table, rows, NT, preferred_element_type=F32)
        new = jnp.maximum(top, jnp.max(s, axis=0, keepdims=True))
        total = total * jnp.exp(top - new) + jnp.sum(jnp.exp(s - new), axis=0, keepdims=True)
        where = lax.broadcasted_iota(jnp.int32, s.shape, 0) == cols - g * table.shape[0]
        hit = hit + jnp.sum(jnp.where(where, s, 0.0), axis=0, keepdims=True)
        return new, total, hit

    zero = jnp.zeros((1, count), F32)
    start = (jnp.full((1, count), -1e30, F32), zero, zero)
    top, total, hit = lax.fori_loop(0, CHUNKS, step, start, unroll=True)
    logs = top + jnp.log(total)
    for p in range(NC):
        here = slice(p * 128, (p + 1) * 128)
        there = pl.ds(pl.multiple_of((k ^ p) * 128, 128), 128)
        for d in range(NC):
            out_ref[d, 0:1, there] = logs[:, here]
            out_ref[d, 1:2, there] = hit[:, here]


def grads_kernel(me_ref, cold_ref, hot_ref, col_ref, stats_ref, *refs):
    *row_refs, keep_ref, send_1, send_2, send_3, out_ref, loss_ref, acc_ref, item_ref, sems = refs
    rows = jnp.concatenate([r[...] for r in row_refs], axis=0)
    cols = col_ref[...]
    k = pick(me_ref[0], COLS)
    pieces = []
    for p in range(NC):
        there = pl.ds(pl.multiple_of((k ^ p) * 128, 128), 128)
        tops = [stats_ref[d, 0:1, there] for d in range(NC)]
        top = functools.reduce(jnp.maximum, tops)
        total = sum(jnp.exp(t - top) for t in tops)
        pieces.append(top + jnp.log(total))
        if p == 0:
            loss_ref[...] = pieces[0] - sum(stats_ref[d, 1:2, there] for d in range(NC))
    logs = jnp.concatenate(pieces, axis=1)
    acc_ref[...] = jnp.zeros_like(acc_ref)
    n = NG // CHUNKS
    cold_rows = cold_ref.shape[1]

    def copy_out(g):
        there = pl.ds(g * n, n)
        return pltpu.make_async_copy(item_ref.at[there], out_ref.at[there], sems.at[g])

    def step(g, carry):
        table = chunk_table(cold_ref, hot_ref, g)
        s = lax.dot_general(table, rows, NT, preferred_element_type=F32)
        where = lax.broadcasted_iota(jnp.int32, s.shape, 0) == cols - g * table.shape[0]
        w = (jnp.exp(s - logs) - jnp.where(where, 1.0, 0.0)).astype(BF)
        item = jnp.dot(w, rows, preferred_element_type=F32).astype(BF)
        wide = item.shape[-1]
        item_ref[pl.ds(g * n, n), :cold_rows] = item[: n * cold_rows].reshape(n, -1, wide)
        item_ref[pl.ds(g * n, n), cold_rows:] = item[n * cold_rows :].reshape(n, -1, wide)
        copy_out(g).start()
        acc_ref[...] += lax.dot_general(table, w, TN, preferred_element_type=F32)
        return carry

    lax.fori_loop(0, CHUNKS, step, 0, unroll=True)
    own = acc_ref.shape[1] // NC
    for j, ref in enumerate((keep_ref, send_1, send_2, send_3)):
        for core in range(2):
            p = core * (NC // 2) + j
            part = acc_ref[:, p * own : (p + 1) * own].T
            ref[core * own : (core + 1) * own] = part.astype(ref.dtype)
    for g in range(CHUNKS):
        copy_out(g).wait()


def place_kernel(me_ref, own_ref, other_ref, keep_ref, out_ref, query_ref, sum_ref, sems):
    core = bit(me_ref[0], "c")
    half = own_ref.shape[0]
    first = pltpu.make_async_copy(own_ref, out_ref.at[pl.ds(core * half, half)], sems.at[0])
    second = pltpu.make_async_copy(
        other_ref.at[pl.ds(0, half)], out_ref.at[pl.ds((1 - core) * half, half)], sems.at[1]
    )
    first.start()
    second.start()
    sum_ref[...] = (keep_ref[...] + other_ref[half:].astype(F32)).astype(sum_ref.dtype)
    third = pltpu.make_async_copy(sum_ref, query_ref, sems.at[2])
    third.start()
    first.wait()
    second.wait()
    third.wait()


def body(queries, hot_table, cold_table, hot_ids, targets):
    own, width = queries.shape
    shard = cold_table.shape[0]
    hot = hot_table.shape[0]
    hot_own = hot // (NC * NG)
    me = lax.axis_index(AXES)
    at_me = jnp.reshape(me, (1,)).astype(jnp.int32)
    k = pick(me, COLS)
    count = NC * own
    params = pltpu.CompilerParams(vmem_limit_bytes=24 << 20)
    vmem = pl.BlockSpec(memory_space=pltpu.VMEM)
    smem = pl.BlockSpec(memory_space=pltpu.SMEM)

    rows = [queries, swap(queries, "z1")]

    column = pl.pallas_call(
        decode_kernel,
        out_shape=jax.ShapeDtypeStruct((1, count), jnp.int32),
        in_specs=[smem, vmem, pl.BlockSpec(memory_space=pltpu.HBM)],
        scratch_shapes=[pltpu.VMEM((1, count), jnp.int32), pltpu.SemaphoreType.DMA((NC,))],
        cost_estimate=pl.CostEstimate(
            flops=6 * hot * count, bytes_accessed=1 << 20, transcendentals=0
        ),
        compiler_params=params,
    )(at_me, hot_ids.reshape(-1, 128), targets.reshape(-1, 1, own))

    far = spread(cold_table, FAR).reshape(NF * shard, width)
    far, rows[1] = lax.optimization_barrier((far, rows[1]))
    cold = spread(far, NEAR)
    rows = jnp.concatenate(rows, axis=0)
    across = swap(rows, "c")
    other, column, across = lax.optimization_barrier((swap(rows, "z2"), column, across))
    rows = [rows, other, across, swap(other, "c")]
    mine = hot_table.reshape(2, NG, NC // 2, hot_own, width)
    mine = lax.dynamic_slice(mine, (k >> 2, 0, k & 3, 0, 0), (1, NG, 1, hot_own, width))
    mine = mine.reshape(NG, hot_own, width)

    stats = pl.pallas_call(
        stats_kernel,
        out_shape=jax.ShapeDtypeStruct((NC, 2, count), F32),
        in_specs=[smem] + [vmem] * (3 + len(rows)),
        compiler_params=params,
    )(at_me, cold, mine, column, *rows)
    stats = lax.all_to_all(stats, COLS, 0, 0)
    keep, *sends, item_part, loss = pl.pallas_call(
        grads_kernel,
        out_shape=(
            jax.ShapeDtypeStruct((count // 4, width), F32),
            *[jax.ShapeDtypeStruct((count // 4, width), BF)] * 3,
            jax.ShapeDtypeStruct((NG, NF * shard + hot_own, width), BF),
            jax.ShapeDtypeStruct((1, own), F32),
        ),
        in_specs=[smem] + [vmem] * (4 + len(rows)),
        out_specs=(vmem, vmem, vmem, vmem, pl.BlockSpec(memory_space=pl.ANY), vmem),
        scratch_shapes=[
            pltpu.VMEM((width, count), F32),
            pltpu.VMEM((NG, NF * shard + hot_own, width), BF),
            pltpu.SemaphoreType.DMA((CHUNKS,)),
        ],
        compiler_params=params,
    )(at_me, cold, mine, column, stats, *rows)

    near = lax.all_to_all(item_part, NEAR, 0, 0)
    keep = keep + sum(x.astype(F32) for x in around(*sends))
    near, keep, other = lax.optimization_barrier((near, keep[:own], keep[own:].astype(BF)))
    near = jnp.sum(near.astype(F32), axis=0).astype(BF)
    cold_part = near[: NF * shard].reshape(NF, shard, width)
    hot_part = jnp.broadcast_to(near[None, NF * shard :], (NF, hot_own, width))
    far = lax.all_to_all(jnp.concatenate([cold_part, hot_part], axis=1), FAR, 0, 0)
    far = jnp.sum(far.astype(F32), axis=0).astype(BF)
    grad_cold = far[:shard]
    grad_hot = spread(far[shard:], HALF).reshape(-1, width)
    grad_hot = spread(grad_hot, NEAR)
    grad_hot = grad_hot.reshape(hot // 2, width)
    swapped = swap(jnp.concatenate([grad_hot, other], axis=0), "c")
    grad_hot, grad_queries = pl.pallas_call(
        place_kernel,
        out_shape=(
            jax.ShapeDtypeStruct((hot, width), BF),
            jax.ShapeDtypeStruct((own, width), BF),
        ),
        in_specs=[smem, vmem, vmem, vmem],
        out_specs=(pl.BlockSpec(memory_space=pl.ANY),) * 2,
        scratch_shapes=[pltpu.VMEM((own, width), BF), pltpu.SemaphoreType.DMA((3,))],
        compiler_params=params,
    )(at_me, grad_hot, swapped, keep)
    return grad_queries, grad_hot, grad_cold, loss[0]


def solution(mesh):
    fine = Mesh(mesh.devices.reshape((2,) * len(AXES)), AXES)
    rows = P(AXES, None)
    return jax.shard_map(
        body,
        mesh=fine,
        in_specs=(rows, P(), rows, P(), P()),
        out_specs=(rows, P(), rows, P(AXES)),
        check_vma=False,
    )
```
